32 devices in a mesh: tm: 8 (over z, x), height: 4 (over y, core).
Axes of the slice: x: 2, y: 2, z: 4, core: 2. Of those that a mesh axis runs over, the one named last changes fastest.
Arguments:
- query_tok: bfloat16 [8, 8, 64, 1536], P('tm', 'height'), may hold values from -6 to 6
- key_tok: bfloat16 [8, 8, 64, 1536], P('tm', 'height'), may hold values from -6 to 6
- value_tok: bfloat16 [8, 8, 64, 1536], P('tm', 'height'), may hold values from -6 to 6
- grad_out: bfloat16 [8, 8, 64, 1536], P('tm', 'height'), may hold values from -6 to 6
- far_picks: int32 [8, 4, 12, 2], P('tm', 'height'), may hold values from 0 to 3
Outputs:
- grad_query: bfloat16 [8, 8, 64, 1536], P('tm', 'height')
- grad_key: bfloat16 [8, 8, 64, 1536], P('tm', 'height')
- grad_value: bfloat16 [8, 8, 64, 1536], P('tm', 'height')
The draws below stay inside these ranges and needn't reach their ends.
All inputs are finite; a program needn't handle non-finite values.
Results may differ from the reference program's by a relative error of at most 0.012.
The reference program's roundings to bfloat16 on the way count: a program that leaves them out, or rounds other values in their place, can miss the bound.
Values may be sent and summed in bfloat16 or wider, within the bound.
No kernel may reach another device: no remote copies, remote signals or barrier semaphores. Data moves between devices by JAX's collectives and lax.ppermute only.
A program may use at most 64 MiB of HBM per device.

```python
import jax
import jax.numpy as jnp
from jax import lax

HEADS = 12
HEAD_DIM = 128
FRAMES_DEV = 1
ROWS_DEV = 2
COLS = 64
REACH = 2
NPICK = 2
WIDTH = 1536
TILES_T = 8
TILES_H = 4
FRAMES = 8
ROWS = 8
TILE = 128
FACE = 64


def base_field(key):
    field = jax.random.truncated_normal(key, -6.0, 6.0, (FRAMES, ROWS, COLS, WIDTH), jnp.float32)
    return field.reshape(TILES_T, FRAMES_DEV, TILES_H, ROWS_DEV, COLS, WIDTH)


def draw_query_tok(key, part):
    field = base_field(jax.random.fold_in(key, 1))
    return field.reshape(FRAMES, ROWS, COLS, WIDTH).astype(jnp.bfloat16)


def draw_key_tok(key, part):
    field = base_field(jax.random.fold_in(key, 2))
    return field.reshape(FRAMES, ROWS, COLS, WIDTH).astype(jnp.bfloat16)


def place_ends(values, own_key, least, largest):
    shape = values.shape
    index_at = [jax.random.randint(jax.random.fold_in(own_key, axis), (), 0, shape[axis]) for axis in range(len(shape))]
    values = values.at[tuple(index_at)].set(least)
    longest = shape.index(max(shape))
    index_at[longest] = (index_at[longest] + 1) % shape[longest]
    return values.at[tuple(index_at)].set(largest)


def shard_levels(own_key, dims, pieces, low, high):
    loudness = 1.0
    for axis_at, parts in pieces:
        draws = jax.random.uniform(jax.random.fold_in(jax.random.fold_in(own_key, 6), axis_at), (parts,), jnp.float32, low / len(pieces), high / len(pieces))
        loudness = loudness * jnp.repeat(jnp.exp(draws), dims[axis_at] // parts).reshape((-1,) + (1,) * (len(dims) - 1 - axis_at))
    return loudness


def gaussian(stream_key, extent, deviation, reach, pieces=(), held_as=jnp.bfloat16):
    drawn = jax.random.normal(stream_key, extent, jnp.float32) * deviation
    if len(pieces) > 0:
        drawn = shard_levels(stream_key, extent, pieces, -0.22, 0.18) * drawn
    return jnp.clip(drawn, min=-reach, max=reach).astype(held_as)


def setup_inputs(seed: int = 0) -> dict:
    keys = jax.random.split(jax.random.key(seed), 6)
    return {
        "query_tok": draw_query_tok(jax.random.fold_in(keys[5], 71), 0),
        "key_tok": draw_key_tok(jax.random.fold_in(keys[5], 71), 0),
        "value_tok": gaussian(keys[2], (FRAMES, ROWS, COLS, WIDTH), 1.0, 6.0, ((0, 8), (1, 4))),
        "grad_out": gaussian(keys[3], (FRAMES, ROWS, COLS, WIDTH), 1.0, 6.0, ((0, 8), (1, 4))),
        "far_picks": place_ends(jax.random.randint(keys[4], (TILES_T, TILES_H, HEADS, NPICK), 0, 2 * REACH), jax.random.fold_in(keys[4], 1), 0, (2 * REACH) - 1).astype(jnp.int32),
    }


def pair_grads(query_rows, key_rows, value_rows, grad_rows, usable):
    score_scale = HEAD_DIM ** -0.5
    query_f = query_rows.astype(jnp.float32)
    key_f = key_rows.astype(jnp.float32)
    value_f = value_rows.astype(jnp.float32)
    grad_f = grad_rows.astype(jnp.float32)
    scores = jnp.einsum('qhd,khd->hqk', query_f, key_f) * score_scale
    scores = jnp.where(usable[:, None, :], scores, -jnp.inf)
    row_top = jnp.max(scores, axis=2, keepdims=True)
    expo = jnp.exp(scores - row_top)
    weights = expo / jnp.sum(expo, axis=2, keepdims=True)
    weights_b = weights.astype(jnp.bfloat16).astype(jnp.float32)
    attended = jnp.einsum('hqk,khd->qhd', weights_b, value_f)
    row_delta = jnp.sum(grad_f * attended, axis=2)
    value_grad = jnp.einsum('hqk,qhd->khd', weights_b, grad_f)
    grad_weights = jnp.einsum('qhd,khd->hqk', grad_f, value_f)
    dscore = (weights * (grad_weights - row_delta.T[:, :, None]) * score_scale).astype(jnp.bfloat16).astype(jnp.float32)
    query_grad = jnp.einsum('hqk,khd->qhd', dscore, key_f)
    key_grad = jnp.einsum('hqk,qhd->khd', dscore, query_f)
    return query_grad, key_grad, value_grad


def to_tiles(field):
    return field.reshape(TILES_T, FRAMES_DEV, TILES_H, ROWS_DEV, COLS, -1).transpose(0, 2, 1, 3, 4, 5)


def from_tiles(field):
    return field.transpose(0, 2, 1, 3, 4, 5).reshape(FRAMES, ROWS, COLS, -1)


def to_bf16_kept(field):
    rounded = field.astype(jnp.bfloat16)
    return lax.optimization_barrier(rounded).astype(jnp.float32)


def reference(query_tok, key_tok, value_tok, grad_out, far_picks):
    offset_list = [shift_by for shift_by in range(-REACH, REACH + 1) if shift_by != 0]
    offset_arr = jnp.array(offset_list, dtype=jnp.int32)
    query_t = to_tiles(query_tok)
    grad_t = to_tiles(grad_out)
    key_value = jnp.concatenate([to_tiles(key_tok), to_tiles(value_tok)], axis=-1)
    tile_pos = jnp.arange(TILES_H, dtype=jnp.int32)
    upper_ok = tile_pos > 0
    lower_ok = tile_pos < TILES_H - 1
    choose = jnp.arange(2 * REACH, dtype=jnp.int32)
    grads_fn = jax.vmap(pair_grads)

    def step(accum, frame_tile):
        own_tile = key_value[frame_tile]
        zero_face = jnp.zeros_like(own_tile[:1, :, ROWS_DEV - 1])
        upper = jnp.concatenate([zero_face, own_tile[:-1, :, ROWS_DEV - 1]], axis=0)
        lower = jnp.concatenate([own_tile[1:, :, 0], zero_face], axis=0)
        blocks = [own_tile.reshape(TILES_H, TILE, 2 * WIDTH), upper.reshape(TILES_H, FACE, 2 * WIDTH), lower.reshape(TILES_H, FACE, 2 * WIDTH)]
        for shift_by in offset_list:
            blocks.append(key_value[(frame_tile + shift_by) % TILES_T].reshape(TILES_H, TILE, 2 * WIDTH))
        stacked = jnp.concatenate(blocks, axis=1)
        total_keys = stacked.shape[1]
        target = frame_tile + offset_arr
        far_ok = (target >= 0) & (target < TILES_T)
        chosen = jnp.any(far_picks[frame_tile][..., None] == choose, axis=2) & far_ok[None, None, :]
        usable = jnp.concatenate([
            jnp.ones((TILES_H, HEADS, TILE), jnp.bool_),
            jnp.broadcast_to(upper_ok[:, None, None], (TILES_H, HEADS, FACE)),
            jnp.broadcast_to(lower_ok[:, None, None], (TILES_H, HEADS, FACE)),
            jnp.repeat(chosen, TILE, axis=2)], axis=2)
        query_grad, key_grad, value_grad = grads_fn(
            query_t[frame_tile].reshape(TILES_H, TILE, HEADS, HEAD_DIM),
            stacked[..., :WIDTH].reshape(TILES_H, total_keys, HEADS, HEAD_DIM),
            stacked[..., WIDTH:].reshape(TILES_H, total_keys, HEADS, HEAD_DIM),
            grad_t[frame_tile].reshape(TILES_H, TILE, HEADS, HEAD_DIM),
            usable)
        key_grads = jnp.concatenate([key_grad.reshape(TILES_H, total_keys, WIDTH), value_grad.reshape(TILES_H, total_keys, WIDTH)], axis=-1)
        own_part = key_grads[:, :TILE].reshape(TILES_H, FRAMES_DEV, ROWS_DEV, COLS, 2 * WIDTH)
        upper_grad = to_bf16_kept(key_grads[:, TILE:TILE + FACE].reshape(TILES_H, FRAMES_DEV, COLS, 2 * WIDTH))
        lower_grad = to_bf16_kept(key_grads[:, TILE + FACE:TILE + 2 * FACE].reshape(TILES_H, FRAMES_DEV, COLS, 2 * WIDTH))
        zero_grad = jnp.zeros_like(upper_grad[:1])
        into_last = jnp.concatenate([upper_grad[1:], zero_grad], axis=0)
        into_first = jnp.concatenate([zero_grad, lower_grad[:-1]], axis=0)
        own_part = own_part.at[:, :, ROWS_DEV - 1].add(into_last).at[:, :, 0].add(into_first)
        accum = accum.at[frame_tile].add(own_part)
        for slot_index, shift_by in enumerate(offset_list):
            start = TILE + 2 * FACE + slot_index * TILE
            rounded = to_bf16_kept(key_grads[:, start:start + TILE])
            accum = accum.at[(frame_tile + shift_by) % TILES_T].add(rounded.reshape(TILES_H, FRAMES_DEV, ROWS_DEV, COLS, 2 * WIDTH))
        return accum, query_grad.reshape(TILES_H, FRAMES_DEV, ROWS_DEV, COLS, WIDTH).astype(jnp.bfloat16)

    start_accum = jnp.zeros((TILES_T, TILES_H, FRAMES_DEV, ROWS_DEV, COLS, 2 * WIDTH), jnp.float32)
    accum, query_grads = lax.scan(step, start_accum, jnp.arange(TILES_T, dtype=jnp.int32))
    grad_query = from_tiles(query_grads)
    grad_key = from_tiles(accum[..., :WIDTH]).astype(jnp.bfloat16)
    grad_value = from_tiles(accum[..., WIDTH:]).astype(jnp.bfloat16)
    return (grad_query, grad_key, grad_value)
```

```python
import functools

import jax
import jax.numpy as jnp
from jax import lax
from jax.experimental import pallas as pl
from jax.experimental.pallas import tpu as pltpu
from jax.sharding import PartitionSpec as P

HEAD_DIM = 128
REACH = 2
SCALE = HEAD_DIM**-0.5
FAR_AWAY = 3e38
VMEM_BYTES = 40 * 1024 * 1024

NT = (((1,), (1,)), ((), ()))
NN = (((1,), (0,)), ((), ()))
TN = (((0,), (0,)), ((), ()))


def dot(left, right, dims):
    return lax.dot_general(left, right, dims, preferred_element_type=jnp.float32)


def routes(size):
    def keep(move):
        return [(i, move(i)) for i in range(size) if 0 <= move(i) < size]

    partner = keep(lambda i: i ^ 1)
    route_a = keep(lambda i: i - 2 if i % 2 == 0 else i + 2)
    route_b = keep(lambda i: i + 2 if i % 2 == 0 else i - 2)
    outer = keep(lambda i: i - 1 if i % 2 == 0 else i + 1)
    return partner, route_a, route_b, outer


def spread(pair, axis):
    size = lax.axis_size(axis)
    partner, route_a, route_b, outer = routes(size)
    from_partner = lax.ppermute(pair, axis, partner)
    from_b = lax.ppermute(pair, axis, route_b)
    from_a = lax.ppermute(pair, axis, route_a)
    if size % 2 == 0:
        first = lax.ppermute(from_partner[0], axis, route_b)
        second = lax.ppermute(from_a[1], axis, partner)
    else:
        first = lax.ppermute(pair[0], axis, outer)
        second = lax.ppermute(pair[1], axis, outer)
    return from_partner, from_a, from_b, first, second


def query_kernel(
    n_tm, n_height, query, grad, own, face_1, face_2, part, a, b, outer_k, outer_v, picks,
    grad_query, own_grads, face_1_grads, face_2_grads, to_part, to_a, to_b, to_outer,
):
    heads = query.shape[1] // HEAD_DIM
    tile, face = query.shape[0], face_1.shape[1]
    at, line = lax.axis_index("tm"), lax.axis_index("height")
    odd, line_odd = lax.rem(at, 2), lax.rem(line, 2)
    slot_part, slot_a, slot_b, slot_outer = 2 - odd, 3 - 3 * odd, 3 * odd, 1 + odd
    slots = (slot_part, slot_a, slot_b, slot_outer)

    def target(slot):
        return at + slot - jnp.where(slot < REACH, REACH, REACH - 1)

    inside = [(target(s) >= 0) & (target(s) < n_tm) for s in slots]
    face_1_ok = (line_odd == 1) | (line + 1 < n_height)
    face_2_ok = jnp.where(line_odd == 1, line + 1 < n_height, line > 0)

    def head(e, carry):
        cols = pl.ds(pl.multiple_of(e * HEAD_DIM, HEAD_DIM), HEAD_DIM)
        q, g = query[:, cols], grad[:, cols]
        keys = [own[0, :, cols], face_1[0, :, cols], face_2[0, :, cols],
                part[0, :, cols], a[0, :, cols], b[0, :, cols], outer_k[:, cols]]
        values = [own[1, :, cols], face_1[1, :, cols], face_2[1, :, cols],
                  part[1, :, cols], a[1, :, cols], b[1, :, cols], outer_v[:, cols]]
        chosen = [ok & ((picks[e, 0] == s) | (picks[e, 1] == s)) for s, ok in zip(slots, inside)]
        present = [None, face_1_ok, face_2_ok] + chosen
        scores = []
        for k, ok in zip(keys, present):
            s = dot(k, q, NT) * SCALE
            scores.append(s if ok is None else s + jnp.where(ok, 0.0, -jnp.inf))
        top = functools.reduce(jnp.maximum, [jnp.max(s, axis=0, keepdims=True) for s in scores])
        expo = [jnp.exp(s - top) for s in scores]
        total = functools.reduce(jnp.add, [jnp.sum(x, axis=0, keepdims=True) for x in expo])
        inverse = 1.0 / total
        weights = [x * inverse for x in expo]
        weights_b = [w.astype(jnp.bfloat16) for w in weights]
        grad_weights = [dot(v, g, NT) for v in values]
        delta = functools.reduce(
            jnp.add,
            [jnp.sum(w.astype(jnp.float32) * x, axis=0, keepdims=True) for w, x in zip(weights_b, grad_weights)],
        )
        dscore = [(w * (x - delta) * SCALE).astype(jnp.bfloat16) for w, x in zip(weights, grad_weights)]
        dq = functools.reduce(jnp.add, [dot(d, k, TN) for d, k in zip(dscore, keys)])
        grad_query[:, cols] = dq.astype(grad_query.dtype)
        own_grads[0, :, cols] = dot(dscore[0], q, NN)
        own_grads[1, :, cols] = dot(weights_b[0], g, NN)
        for out, at_key in ((face_1_grads, 1), (face_2_grads, 2)):
            out[0, :, cols] = dot(dscore[at_key], q, NN).astype(out.dtype)
            out[1, :, cols] = dot(weights_b[at_key], g, NN).astype(out.dtype)
        level = top + jnp.log(total)
        for out, ok in ((to_part, chosen[0]), (to_a, chosen[2]), (to_b, chosen[1]), (to_outer, chosen[3])):
            out[pl.ds(e, 1), :] = jnp.where(ok, level, FAR_AWAY)
            out[pl.ds(e + heads, 1), :] = delta
        return carry

    lax.fori_loop(0, heads, head, 0, unroll=False)


def key_kernel(
    keys, own_grads, face_1_grads, face_2_grads, part, a, b, outer_q, outer_g,
    of_part, of_a, of_b, of_outer, grad_key, grad_value,
):
    heads = keys.shape[2] // HEAD_DIM
    tile, face = keys.shape[1], face_1_grads.shape[1]
    last_first = lax.rem(lax.axis_index("height"), 2) == 0

    def head(e, carry):
        cols = pl.ds(pl.multiple_of(e * HEAD_DIM, HEAD_DIM), HEAD_DIM)
        k, v = keys[0, :, cols], keys[1, :, cols]
        sums = [own_grads[0, :, cols], own_grads[1, :, cols]]
        pairs = [(r[0, :, cols], r[1, :, cols], s) for r, s in ((part, of_part), (a, of_a), (b, of_b))]
        pairs.append((outer_q[:, cols], outer_g[:, cols], of_outer))
        for q, g, stats in pairs:
            level, delta = stats[pl.ds(e, 1), :], stats[pl.ds(e + heads, 1), :]
            weights = jnp.exp(dot(k, q, NT) * SCALE - level)
            grad_weights = dot(v, g, NT)
            dscore = (weights * (grad_weights - delta) * SCALE).astype(jnp.bfloat16)
            sums[0] += dot(dscore, q, NN).astype(jnp.bfloat16).astype(jnp.float32)
            sums[1] += dot(weights.astype(jnp.bfloat16), g, NN).astype(jnp.bfloat16).astype(jnp.float32)
        for at, out in ((0, grad_key), (1, grad_value)):
            one = face_1_grads[at, :, cols].astype(jnp.float32)
            two = face_2_grads[at, :, cols].astype(jnp.float32)
            first = jnp.where(last_first, two, one)
            last = jnp.where(last_first, one, two)
            out[:face, cols] = (sums[at][:face] + first).astype(out.dtype)
            out[face:, cols] = (sums[at][face:] + last).astype(out.dtype)
        return carry

    lax.fori_loop(0, heads, head, 0, unroll=False)


def per_device(query_tok, key_tok, value_tok, grad_out, far_picks):
    frames_dev, rows_dev, columns, width = query_tok.shape
    tile, face = frames_dev * rows_dev * columns, frames_dev * columns
    heads = width // HEAD_DIM
    n_tm, n_height = lax.axis_size("tm"), lax.axis_size("height")
    query, key = query_tok.reshape(tile, width), key_tok.reshape(tile, width)
    value, grad = value_tok.reshape(tile, width), grad_out.reshape(tile, width)
    key_value = jnp.stack([key, value])
    query_grad = jnp.stack([query, grad])
    line_odd = lax.rem(lax.axis_index("height"), 2)
    rows = key_value.reshape(2, rows_dev, face, width)
    pairs_1 = [(i, i ^ 1) for i in range(n_height) if i ^ 1 < n_height]
    pairs_2 = [(i, i - 1 if i % 2 == 0 else i + 1) for i in range(n_height)]
    pairs_2 = [(i, j) for i, j in pairs_2 if 0 <= j < n_height]
    first_row, last_row = rows[:, 0], rows[:, rows_dev - 1]
    face_1 = lax.ppermute(jnp.where(line_odd == 0, last_row, first_row), "height", pairs_1)
    face_2 = lax.ppermute(jnp.where(line_odd == 0, first_row, last_row), "height", pairs_2)
    kv_part, kv_a, kv_b, outer_k, outer_v = spread(key_value, "tm")
    qg_part, qg_a, qg_b, outer_q, outer_g = spread(query_grad, "tm")

    f32, bf16 = jnp.float32, jnp.bfloat16
    vmem = pl.BlockSpec(memory_space=pltpu.VMEM)
    stats = jax.ShapeDtypeStruct((2 * heads, tile), f32)
    block = 2 * tile * tile * HEAD_DIM * heads
    grad_query, own_grads, face_1_grads, face_2_grads, to_part, to_a, to_b, to_outer = pl.pallas_call(
        functools.partial(query_kernel, n_tm, n_height),
        out_shape=(
            jax.ShapeDtypeStruct((tile, width), bf16),
            jax.ShapeDtypeStruct((2, tile, width), f32),
            jax.ShapeDtypeStruct((2, face, width), bf16),
            jax.ShapeDtypeStruct((2, face, width), bf16),
            stats, stats, stats, stats,
        ),
        in_specs=[vmem] * 10 + [pl.BlockSpec(memory_space=pltpu.SMEM)],
        out_specs=[vmem] * 8,
        compiler_params=pltpu.CompilerParams(vmem_limit_bytes=VMEM_BYTES),
        cost_estimate=pl.CostEstimate(flops=22 * block, bytes_accessed=8 << 20, transcendentals=0),
        name="query_side",
    )(query, grad, key_value, face_1, face_2, kv_part, kv_a, kv_b, outer_k, outer_v,
      far_picks.reshape(heads, far_picks.shape[3]))

    partner, route_a, route_b, outer = routes(n_tm)
    of_part = lax.ppermute(to_part, "tm", partner)
    of_a = lax.ppermute(to_a, "tm", route_a)
    of_b = lax.ppermute(to_b, "tm", route_b)
    of_outer = lax.ppermute(to_outer, "tm", outer)
    back_1 = lax.ppermute(face_1_grads, "height", pairs_1)
    back_2 = lax.ppermute(face_2_grads, "height", pairs_2)

    grad_key, grad_value = pl.pallas_call(
        key_kernel,
        out_shape=(jax.ShapeDtypeStruct((tile, width), bf16),) * 2,
        in_specs=[vmem] * 13,
        out_specs=[vmem] * 2,
        compiler_params=pltpu.CompilerParams(vmem_limit_bytes=VMEM_BYTES),
        cost_estimate=pl.CostEstimate(flops=16 * block, bytes_accessed=8 << 20, transcendentals=0),
        name="key_side",
    )(key_value, own_grads, back_1, back_2, qg_part, qg_a, qg_b, outer_q, outer_g,
      of_part, of_a, of_b, of_outer)
    return tuple(x.reshape(query_tok.shape) for x in (grad_query, grad_key, grad_value))


def solution(mesh):
    spec = P("tm", "height", None, None)
    return jax.shard_map(
        per_device, mesh=mesh, in_specs=(spec,) * 5, out_specs=(spec,) * 3, check_vma=False
    )
```

```python
import functools

import jax
import jax.numpy as jnp
from jax import lax
from jax.experimental import pallas as pl
from jax.experimental.pallas import tpu as pltpu
from jax.sharding import PartitionSpec as P

HEAD_DIM = 128
REACH = 2
SCALE = HEAD_DIM**-0.5
LOG2E = 1.4426950408889634
FAR_AWAY = 3e38
VMEM_BYTES = 10 * 1024 * 1024
NT = (((1,), (1,)), ((), ()))
NN = (((1,), (0,)), ((), ()))
TN = (((0,), (0,)), ((), ()))


def dot(left, right, dims):
    return lax.dot_general(left, right, dims, preferred_element_type=jnp.float32)


def corners(first, second):
    zero = jnp.zeros_like(first)
    top = jnp.concatenate([first, zero], axis=1)
    return jnp.concatenate([top, jnp.concatenate([zero, second], axis=1)], axis=0)


def routes(size):
    def keep(move):
        return [(i, move(i)) for i in range(size) if 0 <= move(i) < size]

    partner = keep(lambda i: i ^ 1)
    route_a = keep(lambda i: i - 2 if i % 2 == 0 else i + 2)
    route_b = keep(lambda i: i + 2 if i % 2 == 0 else i - 2)
    outer = keep(lambda i: i - 1 if i % 2 == 0 else i + 1)
    return partner, route_a, route_b, outer


def after(value, *done):
    return lax.optimization_barrier((value, *done))[0]


class Either:
    def __init__(self, second, if_second, if_first):
        self.second, self.if_second, self.if_first = second == 1, if_second, if_first
        self.shape = if_first.shape

    def __getitem__(self, at):
        return jnp.where(self.second, self.if_second[at], self.if_first[at])


def query_kernel(
    n_tm, n_height, mine, own, face_1, face_2, part, a, b, outer_even, outer_odd, picks,
    grad_query, own_grads, face_1_grads, face_2_grads, stats, scores,
):
    query, grad = mine.at[0], mine.at[1]
    heads = query.shape[1] // HEAD_DIM
    at, line = lax.axis_index("tm"), lax.axis_index("height")
    odd, line_odd = lax.rem(at, 2), lax.rem(line, 2)
    slots = (2 - odd, 3 - 3 * odd, 3 * odd, 1 + odd)

    def inside(slot):
        target = at + slot - jnp.where(slot < REACH, REACH, REACH - 1)
        return (target >= 0) & (target < n_tm)

    slot_ok = [inside(s) for s in slots]
    face_1_ok = (line_odd == 1) | (line + 1 < n_height)
    face_2_ok = jnp.where(line_odd == 1, line + 1 < n_height, line > 0)
    row_1, row_2 = line_odd, 1 - line_odd
    sets = [(own.at[0], own.at[1])]
    sets += [(f.at[0, r], f.at[1, r]) for f, r in ((face_1, row_1), (face_2, row_2))]
    sets += [(x.at[0], x.at[1]) for x in (part, a, b)]
    sets += [tuple(Either(line_odd, outer_odd.at[i], outer_even.at[i]) for i in (0, 1))]
    spans, start = [], 0
    for keys, _ in sets:
        spans.append(pl.ds(start, keys.shape[0]))
        start += keys.shape[0]

    def columns(e):
        return pl.ds(e * HEAD_DIM, HEAD_DIM)

    def products(e):
        cols = columns(e)
        both = corners(query[:, cols], grad[:, cols])
        for (keys, values), span in zip(sets, spans):
            pair = jnp.concatenate([keys[:, cols], values[:, cols]], axis=1)
            scores[e % 2, span, :] = dot(pair, both, NT)

    def finish(e):
        cols = columns(e)
        q, g = query[:, cols], grad[:, cols]
        chosen = [ok & ((picks[e, 0] == s) | (picks[e, 1] == s)) for s, ok in zip(slots, slot_ok)]
        present = [None, face_1_ok, face_2_ok] + chosen
        score = [scores.at[e % 2, span, pl.ds(0, HEAD_DIM)] for span in spans]
        grad_weight = [scores.at[e % 2, span, pl.ds(HEAD_DIM, HEAD_DIM)] for span in spans]
        tops = [jnp.max(s[...], axis=0, keepdims=True) for s in score]
        tops = [t if ok is None else jnp.where(ok, t, -jnp.inf) for t, ok in zip(tops, present)]
        top = functools.reduce(jnp.maximum, tops) * (SCALE * LOG2E)
        expo = [
            jnp.exp2(s[...] * (SCALE * LOG2E) - (top if ok is None else jnp.where(ok, top, FAR_AWAY)))
            for s, ok in zip(score, present)
        ]
        total = sum(jnp.sum(x, axis=0, keepdims=True) for x in expo)
        inverse = 1.0 / total
        delta = sum(jnp.sum(x * w[...], axis=0, keepdims=True) for x, w in zip(expo, grad_weight))
        delta = delta * inverse
        level = top + jnp.log2(total)
        stats[0, e : e + 1, :] = delta
        for i, ok in enumerate(chosen):
            stats[1 + i, e : e + 1, :] = jnp.where(ok, level, FAR_AWAY)
        weights = [x * inverse for x in expo]
        dscore = [
            (w * (x[...] - delta) * SCALE).astype(jnp.bfloat16) for w, x in zip(weights, grad_weight)
        ]
        all_keys = jnp.concatenate([keys[:, cols] for keys, _ in sets], axis=0)
        dq = dot(jnp.concatenate(dscore, axis=0), all_keys, TN)
        grad_query[:, cols] = dq.astype(grad_query.dtype)
        both = corners(q, g)
        for i, out in enumerate((own_grads, face_1_grads, face_2_grads)):
            pair = jnp.concatenate([dscore[i], weights[i].astype(jnp.bfloat16)], axis=1)
            grads = dot(pair, both, NN)
            out[0, :, cols] = grads[:, :HEAD_DIM].astype(out.dtype)
            out[1, :, cols] = grads[:, HEAD_DIM:].astype(out.dtype)

    products(0)
    for e in range(heads):
        if e + 1 < heads:
            products(e + 1)
        finish(e)


def far_grads(keys, pairs, sums, store, scratch):
    heads = keys.shape[2] // HEAD_DIM

    def columns(e):
        return pl.ds(e * HEAD_DIM, HEAD_DIM)

    def products(e):
        cols = columns(e)
        pair = jnp.concatenate([keys[0, :, cols], keys[1, :, cols]], axis=1)
        for i, (query, grad, _, _) in enumerate(pairs):
            scratch[e % 2, i] = dot(pair, corners(query[:, cols], grad[:, cols]), NT)

    def finish(e):
        cols = columns(e)
        total = sums(cols)
        for i, (query, grad, levels, deltas) in enumerate(pairs):
            score, grad_weights = scratch.at[e % 2, i, :, :HEAD_DIM], scratch.at[e % 2, i, :, HEAD_DIM:]
            weights = jnp.exp2(score[...] * (SCALE * LOG2E) - levels[e : e + 1, :])
            dscore = weights * (grad_weights[...] - deltas[e : e + 1, :]) * SCALE
            both = jnp.concatenate([dscore.astype(jnp.bfloat16), weights.astype(jnp.bfloat16)], axis=1)
            total += dot(both, corners(query[:, cols], grad[:, cols]), NN)
        store(cols, total)

    products(0)
    for e in range(heads):
        if e + 1 < heads:
            products(e + 1)
        finish(e)


def key_kernel(keys, own_grads, part, a, of_part, of_a, sums_out, scratch):
    def sums(cols):
        return jnp.concatenate([own_grads[0, :, cols], own_grads[1, :, cols]], axis=1)

    def store(cols, total):
        sums_out[0, :, cols] = total[:, :HEAD_DIM]
        sums_out[1, :, cols] = total[:, HEAD_DIM:]

    pairs = (
        (part.at[0], part.at[1], of_part.at[1], of_part.at[0]),
        (a.at[0], a.at[1], of_a.at[3], of_a.at[0]),
    )
    far_grads(keys, pairs, sums, store, scratch)


def last_kernel(
    keys, sums_in, face_1_grads, face_2_grads, b, outer_even, outer_odd, of_b, grad_key, grad_value,
    scratch,
):
    face = face_1_grads.shape[1]
    line_odd = lax.rem(lax.axis_index("height"), 2)
    last_first = line_odd == 0
    outer = [Either(line_odd, outer_odd.at[i], outer_even.at[i]) for i in (0, 1)]

    def sums(cols):
        return jnp.concatenate([sums_in[0, :, cols], sums_in[1, :, cols]], axis=1)

    def store(cols, total):
        for at, out in ((0, grad_key), (1, grad_value)):
            one = face_1_grads[at, :, cols].astype(jnp.float32)
            two = face_2_grads[at, :, cols].astype(jnp.float32)
            first, last = jnp.where(last_first, two, one), jnp.where(last_first, one, two)
            part = total[:, at * HEAD_DIM : (at + 1) * HEAD_DIM]
            out[:face, cols] = (part[:face] + first).astype(out.dtype)
            out[face:, cols] = (part[face:] + last).astype(out.dtype)

    pairs = (
        (b.at[0], b.at[1], of_b.at[0, 2], of_b.at[0, 0]),
        (*outer, of_b.at[1, 4], of_b.at[1, 0]),
    )
    far_grads(keys, pairs, sums, store, scratch)


def per_device(query_tok, key_tok, value_tok, grad_out, far_picks):
    frames_dev, rows_dev, columns, width = query_tok.shape
    tile, face = frames_dev * rows_dev * columns, frames_dev * columns
    heads = width // HEAD_DIM
    n_tm, n_height = lax.axis_size("tm"), lax.axis_size("height")
    query, key = query_tok.reshape(tile, width), key_tok.reshape(tile, width)
    value, grad = value_tok.reshape(tile, width), grad_out.reshape(tile, width)
    partner, route_a, route_b, outer = routes(n_tm)

    def move(block, route):
        return lax.ppermute(block, "tm", route)

    def relay(own, from_partner, from_a):
        if n_tm % 2:
            return (move(own, outer),) * 2

        def of_line(route, odd):
            lines = range(odd, n_height, 2)
            return [(i * n_height + h, j * n_height + h) for h in lines for i, j in route]

        even = lax.ppermute(from_partner, ("tm", "height"), of_line(route_b, 0))
        return even, lax.ppermute(from_a, ("tm", "height"), of_line(partner, 1))

    pairs_1 = [(i, i ^ 1) for i in range(n_height) if i ^ 1 < n_height]
    pairs_2 = [(i, i - 1 if i % 2 == 0 else i + 1) for i in range(n_height)]
    pairs_2 = [(i, j) for i, j in pairs_2 if 0 <= j < n_height]

    key_value, query_grad = jnp.stack([key, value]), jnp.stack([query, grad])
    kv_part, kv_a, kv_b = move(key_value, partner), move(key_value, route_a), move(key_value, route_b)
    face_1 = lax.ppermute(key_value, "height", pairs_1)
    face_2 = lax.ppermute(key_value, "height", pairs_2)
    kv_even, kv_odd = relay(key_value, kv_part, kv_a)
    qg_part = move(after(query_grad, kv_a), partner)
    qg_a = move(after(query_grad, kv_a), route_a)
    qg_b = move(after(query_grad, kv_part), route_b)

    f32, bf16 = jnp.float32, jnp.bfloat16
    vmem = pl.BlockSpec(memory_space=pltpu.VMEM)
    block = 2 * tile * tile * HEAD_DIM * heads
    total_keys = tile * (1 + 2 * REACH) + 2 * face
    params = pltpu.CompilerParams(vmem_limit_bytes=VMEM_BYTES)
    by_row = (2, rows_dev, face, width)
    grad_query, own_grads, face_1_grads, face_2_grads, stats = pl.pallas_call(
        functools.partial(query_kernel, n_tm, n_height),
        out_shape=(
            jax.ShapeDtypeStruct((tile, width), bf16),
            jax.ShapeDtypeStruct((2, tile, width), f32),
            jax.ShapeDtypeStruct((2, face, width), bf16),
            jax.ShapeDtypeStruct((2, face, width), bf16),
            jax.ShapeDtypeStruct((1 + 2 * REACH, heads, tile), f32),
        ),
        in_specs=[vmem] * 9 + [pl.BlockSpec(memory_space=pltpu.SMEM)],
        out_specs=[vmem] * 5,
        scratch_shapes=[pltpu.VMEM((2, total_keys, 2 * HEAD_DIM), f32)],
        compiler_params=params,
        cost_estimate=pl.CostEstimate(flops=22 * block, bytes_accessed=8 << 20, transcendentals=0),
        name="query_side",
    )(query_grad, key_value, face_1.reshape(by_row), face_2.reshape(by_row), kv_part, kv_a, kv_b,
      kv_even, kv_odd, far_picks.reshape(heads, far_picks.shape[3]))

    of_part, of_a = move(stats, partner), move(stats, route_a)
    qg_even, qg_odd = relay(query_grad, after(qg_part, of_part), after(qg_a, stats))
    of_b = move(jnp.stack([stats, of_part]), route_b)
    if n_tm % 2:
        of_b = jnp.stack([of_b[0], move(stats, outer)])
    back_1 = lax.ppermute(face_1_grads, "height", pairs_1)
    back_2 = lax.ppermute(face_2_grads, "height", pairs_2)

    scratch = [pltpu.VMEM((2, 2, tile, 2 * HEAD_DIM), f32)]
    sums = pl.pallas_call(
        key_kernel,
        out_shape=jax.ShapeDtypeStruct((2, tile, width), f32),
        in_specs=[vmem] * 6,
        out_specs=vmem,
        scratch_shapes=scratch,
        compiler_params=params,
        cost_estimate=pl.CostEstimate(flops=8 * block, bytes_accessed=8 << 20, transcendentals=0),
        name="key_side",
    )(key_value, own_grads, qg_part, qg_a, of_part, of_a)
    grad_key, grad_value = pl.pallas_call(
        last_kernel,
        out_shape=(jax.ShapeDtypeStruct((tile, width), bf16),) * 2,
        in_specs=[vmem] * 8,
        out_specs=[vmem] * 2,
        scratch_shapes=scratch,
        compiler_params=params,
        cost_estimate=pl.CostEstimate(flops=8 * block, bytes_accessed=8 << 20, transcendentals=0),
        name="last_side",
    )(key_value, sums, back_1, back_2, qg_b, qg_even, qg_odd, of_b)
    return tuple(x.reshape(query_tok.shape) for x in (grad_query, grad_key, grad_value))


def solution(mesh):
    spec = P("tm", "height", None, None)
    return jax.shard_map(
        per_device, mesh=mesh, in_specs=(spec,) * 5, out_specs=(spec,) * 3, check_vma=False
    )
```

```python
import functools

import jax
import jax.numpy as jnp
from jax import lax
from jax.experimental import pallas as pl
from jax.experimental.pallas import tpu as pltpu
from jax.sharding import PartitionSpec as P

HEAD_DIM = 128
REACH = 2
SCALE = HEAD_DIM**-0.5
LOG2E = 1.4426950408889634
FAR_AWAY = 3e38
VMEM_BYTES = 12 * 1024 * 1024
NT = (((1,), (1,)), ((), ()))
NN = (((1,), (0,)), ((), ()))
TN = (((0,), (0,)), ((), ()))


def dot(left, right, dims):
    return lax.dot_general(left, right, dims, preferred_element_type=jnp.float32)


def corners(first, second):
    zero = jnp.zeros_like(first)
    top = jnp.concatenate([first, zero], axis=1)
    return jnp.concatenate([top, jnp.concatenate([zero, second], axis=1)], axis=0)


def columns(e):
    return pl.ds(e * HEAD_DIM, HEAD_DIM)


def routes(size):
    def keep(move):
        return [(i, move(i)) for i in range(size) if 0 <= move(i) < size]

    partner = keep(lambda i: i ^ 1)
    route_a = keep(lambda i: i - 2 if i % 2 == 0 else i + 2)
    route_b = keep(lambda i: i + 2 if i % 2 == 0 else i - 2)
    outer = keep(lambda i: i - 1 if i % 2 == 0 else i + 1)
    return partner, route_a, route_b, outer


def after(value, *done):
    return lax.optimization_barrier((value, *done))[0]


def in_hbm(block):
    return pltpu.with_memory_space_constraint(block, pltpu.HBM)


def pair_kernel(key, value, query, grad, key_value, query_grad, sems):
    parts = sems.shape[1]
    rows = key.shape[0] // parts
    copies = []
    for i, (source, out) in enumerate(
        ((key, key_value.at[0]), (value, key_value.at[1]), (query, query_grad.at[0]), (grad, query_grad.at[1]))
    ):
        for part in range(parts):
            at = pl.ds(part * rows, rows)
            copies.append(pltpu.make_async_copy(source.at[at], out.at[at], sems.at[i, part]))
    for copy in copies:
        copy.start()
    for copy in copies:
        copy.wait()


def paired(*blocks):
    rows, width = blocks[0].shape
    parts = 4 if rows % 64 == 0 else 1
    return pl.pallas_call(
        pair_kernel,
        out_shape=(jax.ShapeDtypeStruct((2, rows, width), blocks[0].dtype),) * 2,
        in_specs=[pl.BlockSpec(memory_space=pltpu.HBM)] * 4,
        out_specs=[pl.BlockSpec(memory_space=pltpu.VMEM)] * 2,
        scratch_shapes=[pltpu.SemaphoreType.DMA((4, parts))],
        compiler_params=pltpu.CompilerParams(vmem_limit_bytes=VMEM_BYTES),
        cost_estimate=pl.CostEstimate(flops=0, bytes_accessed=16 * rows * width, transcendentals=0),
        name="pairs",
    )(*map(in_hbm, blocks))


class Stream:
    def __init__(self, sources, buffers, sems):
        heads = buffers[0].shape[2] // HEAD_DIM
        self.chunks = sems.shape[0]
        self.step = heads // self.chunks
        self.sources, self.buffers, self.sems = sources, buffers, sems
        for chunk in range(self.chunks):
            for i in range(len(sources)):
                self.copy(chunk, i).start()

    def copy(self, chunk, i):
        cols = pl.ds(chunk * self.step * HEAD_DIM, self.step * HEAD_DIM)
        return pltpu.make_async_copy(
            self.sources[i].at[:, :, cols], self.buffers[i].at[:, :, cols], self.sems.at[chunk, i]
        )

    def ready(self, e):
        if e % self.step == 0:
            for i in range(len(self.sources)):
                self.copy(e // self.step, i).wait()


def stream_sems(heads, count):
    return pltpu.SemaphoreType.DMA((4 if heads % 4 == 0 else 1, count))


def query_kernel(
    n_tm, n_height, mine, own, face_1, face_2, part, a, b, outer, picks,
    grad_query, own_grads, face_1_grads, face_2_grads, stats,
    scratch, graded, face_1_vmem, face_2_vmem, far_vmem, sems,
):
    heads, n_picks = mine.shape[2] // HEAD_DIM, picks.shape[1]
    at, line = lax.axis_index("tm"), lax.axis_index("height")
    odd, line_odd = lax.rem(at, 2), lax.rem(line, 2)
    sources = (face_1.at[:, line_odd], face_2.at[:, 1 - line_odd], part, a, b, outer)
    buffers = (face_1_vmem, face_2_vmem, *(far_vmem.at[i] for i in range(2 * REACH)))
    stream = Stream(sources, buffers, sems)
    query, grad = mine.at[0], mine.at[1]
    face_1_ok = (line_odd == 1) | (line + 1 < n_height)
    face_2_ok = jnp.where(line_odd == 1, line + 1 < n_height, line > 0)
    slot_at = (2 - odd, 3 - 3 * odd, 3 * odd, 1 + odd)
    rows = [own.shape[1], face_1_vmem.shape[1], face_2_vmem.shape[1]] + [own.shape[1]] * n_picks
    spans = [pl.ds(sum(rows[:i]), count) for i, count in enumerate(rows)]
    left, right = pl.ds(0, HEAD_DIM), pl.ds(HEAD_DIM, HEAD_DIM)

    def chosen(e, p):
        slot = picks[e, p]
        target = at + slot - jnp.where(slot < REACH, REACH, REACH - 1)
        ok = (target >= 0) & (target < n_tm)
        for before in range(p):
            ok &= picks[e, before] != slot
        return ok

    def place(e, p):
        return sum(jnp.where(picks[e, p] == slot, i, 0) for i, slot in enumerate(slot_at))

    def blocks(e, which):
        cols = columns(e)
        far = [far_vmem[place(e, p), which, :, cols] for p in range(n_picks)]
        return [own[which, :, cols], face_1_vmem[which, :, cols], face_2_vmem[which, :, cols], *far]

    def products(e):
        stream.ready(e)
        both = corners(query[:, columns(e)], grad[:, columns(e)])
        for key, value, span in zip(blocks(e, 0), blocks(e, 1), spans):
            scratch[e % 2, span, :] = dot(jnp.concatenate([key, value], axis=1), both, NT)

    def softmax(e):
        present = [None, face_1_ok, face_2_ok] + [chosen(e, p) for p in range(n_picks)]
        score = [scratch.at[e % 2, span, left] for span in spans]
        grad_weight = [scratch.at[e % 2, span, right] for span in spans]
        tops = [jnp.max(s[...], axis=0, keepdims=True) for s in score]
        tops = [t if ok is None else jnp.where(ok, t, -jnp.inf) for t, ok in zip(tops, present)]
        top = functools.reduce(jnp.maximum, tops) * (SCALE * LOG2E)
        expo = [
            jnp.exp2(s[...] * (SCALE * LOG2E) - (top if ok is None else jnp.where(ok, top, FAR_AWAY)))
            for s, ok in zip(score, present)
        ]
        total = sum(jnp.sum(x, axis=0, keepdims=True) for x in expo)
        inverse = 1.0 / total
        delta = sum(jnp.sum(x * w[...], axis=0, keepdims=True) for x, w in zip(expo, grad_weight))
        delta, level = delta * inverse, top + jnp.log2(total)
        stats[0, e : e + 1, :] = delta
        for i, slot in enumerate(slot_at):
            ok = [present[3 + p] & (picks[e, p] == slot) for p in range(n_picks)]
            stats[1 + i, e : e + 1, :] = jnp.where(functools.reduce(jnp.logical_or, ok), level, FAR_AWAY)
        for i, (x, w, span) in enumerate(zip(expo, grad_weight, spans)):
            weights = x * inverse
            graded[e % 2, span, left] = (weights * (w[...] - delta) * SCALE).astype(jnp.bfloat16)
            if i < 3:
                graded[e % 2, span, right] = weights.astype(jnp.bfloat16)

    def gradients(e):
        cols = columns(e)
        dq = dot(graded[e % 2, :, left], jnp.concatenate(blocks(e, 0), axis=0), TN)
        grad_query[:, cols] = dq.astype(grad_query.dtype)
        both = corners(query[:, cols], grad[:, cols])
        for out, span in zip((own_grads, face_1_grads, face_2_grads), spans):
            grads = dot(graded[e % 2, span, :], both, NN)
            out[0, :, cols] = grads[:, :HEAD_DIM].astype(out.dtype)
            out[1, :, cols] = grads[:, HEAD_DIM:].astype(out.dtype)

    for step in range(heads + 2):
        if step < heads:
            products(step)
        if 0 <= step - 1 < heads:
            softmax(step - 1)
        if 0 <= step - 2:
            gradients(step - 2)


def key_kernel(
    keys, own_grads, face_1_grads, face_2_grads, part, a, b, outer, of_part, of_a, of_b,
    grad_key, grad_value, scratch,
):
    heads, face = keys.shape[2] // HEAD_DIM, face_1_grads.shape[1]
    last_first = lax.rem(lax.axis_index("height"), 2) == 0
    others = ((part, of_part.at[0], 1), (a, of_a, 3), (b, of_b, 2), (outer, of_part.at[1], 4))

    def products(e):
        cols = columns(e)
        pair = jnp.concatenate([keys[0, :, cols], keys[1, :, cols]], axis=1)
        for i, (block, _, _) in enumerate(others):
            scratch[e % 2, i] = dot(pair, corners(block[0, :, cols], block[1, :, cols]), NT)

    def finish(e):
        cols = columns(e)
        sums = jnp.concatenate([own_grads[0, :, cols], own_grads[1, :, cols]], axis=1)
        for i, (block, stats, slot) in enumerate(others):
            score, grad_weights = scratch[e % 2, i, :, :HEAD_DIM], scratch[e % 2, i, :, HEAD_DIM:]
            weights = jnp.exp2(score * (SCALE * LOG2E) - stats[slot, e : e + 1, :])
            dscore = weights * (grad_weights - stats[0, e : e + 1, :]) * SCALE
            both = jnp.concatenate([dscore.astype(jnp.bfloat16), weights.astype(jnp.bfloat16)], axis=1)
            sums += dot(both, corners(block[0, :, cols], block[1, :, cols]), NN)
        for at, out in ((0, grad_key), (1, grad_value)):
            one = face_1_grads[at, :, cols].astype(jnp.float32)
            two = face_2_grads[at, :, cols].astype(jnp.float32)
            first, last = jnp.where(last_first, two, one), jnp.where(last_first, one, two)
            part_sum = sums[:, at * HEAD_DIM : (at + 1) * HEAD_DIM]
            out[:face, cols] = (part_sum[:face] + first).astype(out.dtype)
            out[face:, cols] = (part_sum[face:] + last).astype(out.dtype)

    products(0)
    for e in range(heads):
        if e + 1 < heads:
            products(e + 1)
        finish(e)


def per_device(query_tok, key_tok, value_tok, grad_out, far_picks):
    frames_dev, rows_dev, columns, width = query_tok.shape
    tile, face = frames_dev * rows_dev * columns, frames_dev * columns
    heads, n_picks = width // HEAD_DIM, far_picks.shape[3]
    n_tm, n_height = lax.axis_size("tm"), lax.axis_size("height")
    query, key = query_tok.reshape(tile, width), key_tok.reshape(tile, width)
    value, grad = value_tok.reshape(tile, width), grad_out.reshape(tile, width)
    partner, route_a, route_b, outer = routes(n_tm)
    relayed = n_tm % 2 == 0
    pairs_1 = [(i, i ^ 1) for i in range(n_height) if i ^ 1 < n_height]
    pairs_2 = [(i, i - 1 if i % 2 == 0 else i + 1) for i in range(n_height)]
    pairs_2 = [(i, j) for i, j in pairs_2 if 0 <= j < n_height]

    def move(block, route):
        return lax.ppermute(block, "tm", route)

    key_value, query_grad = paired(key, value, query, grad)
    kv_part, kv_b = move(key_value, partner), move(key_value, route_b)
    kv_a = move(after(key_value, kv_part), route_a)
    face_1 = lax.ppermute(key_value, "height", pairs_1)
    face_2 = lax.ppermute(key_value, "height", pairs_2)
    qg_part = move(after(query_grad, kv_part), partner)
    qg_a = move(query_grad, route_a)
    kv_outer = move(after(kv_part, face_1, face_2), route_b) if relayed else move(key_value, outer)
    qg_b = move(after(query_grad, kv_b), route_b)
    qg_outer = move(qg_a, partner) if relayed else move(query_grad, outer)

    f32, bf16 = jnp.float32, jnp.bfloat16
    vmem, hbm = pl.BlockSpec(memory_space=pltpu.VMEM), pl.BlockSpec(memory_space=pltpu.HBM)
    block = 2 * tile * tile * HEAD_DIM * heads
    params = pltpu.CompilerParams(vmem_limit_bytes=VMEM_BYTES)
    by_row = (2, rows_dev, face, width)
    grad_query, own_grads, face_1_grads, face_2_grads, stats = pl.pallas_call(
        functools.partial(query_kernel, n_tm, n_height),
        out_shape=(
            jax.ShapeDtypeStruct((tile, width), bf16),
            jax.ShapeDtypeStruct((2, tile, width), f32),
            jax.ShapeDtypeStruct((2, face, width), bf16),
            jax.ShapeDtypeStruct((2, face, width), bf16),
            jax.ShapeDtypeStruct((1 + 2 * REACH, heads, tile), f32),
        ),
        in_specs=[vmem] * 2 + [hbm] * 6 + [pl.BlockSpec(memory_space=pltpu.SMEM)],
        out_specs=[vmem] * 5,
        scratch_shapes=[
            pltpu.VMEM((2, tile * (1 + n_picks) + 2 * face, 2 * HEAD_DIM), f32),
            pltpu.VMEM((2, tile * (1 + n_picks) + 2 * face, 2 * HEAD_DIM), bf16),
            *[pltpu.VMEM((2, face, width), bf16)] * 2,
            pltpu.VMEM((2 * REACH, 2, tile, width), bf16),
            stream_sems(heads, 2 + 2 * REACH),
        ],
        compiler_params=params,
        cost_estimate=pl.CostEstimate(flops=200 * block, bytes_accessed=4 << 20, transcendentals=0),
        name="query_side",
    )(query_grad, key_value, in_hbm(face_1.reshape(by_row)), in_hbm(face_2.reshape(by_row)),
      in_hbm(kv_part), in_hbm(kv_a), in_hbm(kv_b), in_hbm(kv_outer),
      far_picks.reshape(heads, n_picks))

    of_a, of_b = move(stats, route_a), move(stats, route_b)
    of_part = move(jnp.stack([stats, of_a]), partner)
    if not relayed:
        of_part = jnp.stack([of_part[0], move(stats, outer)])
    back_1 = lax.ppermute(face_1_grads, "height", pairs_1)
    back_2 = lax.ppermute(face_2_grads, "height", pairs_2)

    grad_key, grad_value = pl.pallas_call(
        key_kernel,
        out_shape=(jax.ShapeDtypeStruct((tile, width), bf16),) * 2,
        in_specs=[vmem] * 11,
        out_specs=[vmem] * 2,
        scratch_shapes=[pltpu.VMEM((2, 2 * REACH, tile, 2 * HEAD_DIM), f32)],
        compiler_params=params,
        cost_estimate=pl.CostEstimate(flops=100 * block, bytes_accessed=4 << 20, transcendentals=0),
        name="key_side",
    )(key_value, own_grads, back_1, back_2, qg_part, qg_a, qg_b, qg_outer, of_part, of_a, of_b)
    return tuple(x.reshape(query_tok.shape) for x in (grad_query, grad_key, grad_value))


def solution(mesh):
    spec = P("tm", "height", None, None)
    return jax.shard_map(
        per_device, mesh=mesh, in_specs=(spec,) * 5, out_specs=(spec,) * 3, check_vma=False
    )
```

```python
import functools

import jax
import jax.numpy as jnp
from jax import lax
from jax.experimental import pallas as pl
from jax.experimental.pallas import tpu as pltpu
from jax.sharding import PartitionSpec as P

HEAD_DIM = 128
REACH = 2
SCALE = HEAD_DIM**-0.5
LOG2E = 1.4426950408889634
FAR_AWAY = 3e38
VMEM_BYTES = 12 * 1024 * 1024
NT = (((1,), (1,)), ((), ()))
NN = (((1,), (0,)), ((), ()))
TN = (((0,), (0,)), ((), ()))


def dot(left, right, dims):
    return lax.dot_general(left, right, dims, preferred_element_type=jnp.float32)


def corners(first, second):
    zero = jnp.zeros_like(first)
    top = jnp.concatenate([first, zero], axis=1)
    return jnp.concatenate([top, jnp.concatenate([zero, second], axis=1)], axis=0)


def columns(e):
    return pl.ds(e * HEAD_DIM, HEAD_DIM)


def routes(size):
    def keep(move):
        return [(i, move(i)) for i in range(size) if 0 <= move(i) < size]

    partner = keep(lambda i: i ^ 1)
    route_a = keep(lambda i: i - 2 if i % 2 == 0 else i + 2)
    route_b = keep(lambda i: i + 2 if i % 2 == 0 else i - 2)
    outer = keep(lambda i: i - 1 if i % 2 == 0 else i + 1)
    return partner, route_a, route_b, outer


def after(value, *done):
    return lax.optimization_barrier((value, *done))[0]


def in_hbm(block):
    return pltpu.with_memory_space_constraint(block, pltpu.HBM)


def pair_kernel(key, value, query, grad, key_value, query_grad, sems):
    parts = sems.shape[1]
    rows = key.shape[0] // parts
    copies = []
    for i, (source, out) in enumerate(
        ((key, key_value.at[0]), (value, key_value.at[1]), (query, query_grad.at[0]), (grad, query_grad.at[1]))
    ):
        for part in range(parts):
            at = pl.ds(part * rows, rows)
            copies.append(pltpu.make_async_copy(source.at[at], out.at[at], sems.at[i, part]))
    for copy in copies:
        copy.start()
    for copy in copies:
        copy.wait()


def paired(*blocks):
    rows, width = blocks[0].shape
    parts = 4 if rows % 64 == 0 else 1
    return pl.pallas_call(
        pair_kernel,
        out_shape=(jax.ShapeDtypeStruct((2, rows, width), blocks[0].dtype),) * 2,
        in_specs=[pl.BlockSpec(memory_space=pltpu.HBM)] * 4,
        out_specs=[pl.BlockSpec(memory_space=pltpu.VMEM)] * 2,
        scratch_shapes=[pltpu.SemaphoreType.DMA((4, parts))],
        compiler_params=pltpu.CompilerParams(vmem_limit_bytes=VMEM_BYTES),
        cost_estimate=pl.CostEstimate(flops=0, bytes_accessed=16 * rows * width, transcendentals=0),
        name="pairs",
    )(*map(in_hbm, blocks))


class Stream:
    def __init__(self, sources, buffers, sems):
        heads = buffers[0].shape[2] // HEAD_DIM
        self.starts = stream_starts(heads)
        self.ends = self.starts[1:] + [heads]
        self.sources, self.buffers, self.sems = sources, buffers, sems
        for chunk in range(len(self.starts)):
            for i in range(len(sources)):
                self.copy(chunk, i).start()

    def copy(self, chunk, i):
        cols = pl.ds(self.starts[chunk] * HEAD_DIM, (self.ends[chunk] - self.starts[chunk]) * HEAD_DIM)
        return pltpu.make_async_copy(
            self.sources[i].at[:, :, cols], self.buffers[i].at[:, :, cols], self.sems.at[chunk, i]
        )

    def ready(self, e):
        if e in self.starts:
            for i in range(len(self.sources)):
                self.copy(self.starts.index(e), i).wait()


def stream_starts(heads):
    return [at for at in (0, 1, 3, 7) if at < heads]


def stream_sems(heads, count):
    return pltpu.SemaphoreType.DMA((len(stream_starts(heads)), count))


def query_kernel(
    n_tm, n_height, mine, own, face_1, face_2, part, a, b, outer, picks,
    grad_query, own_grads, face_1_grads, face_2_grads, stats,
    scratch, graded, face_1_vmem, face_2_vmem, far_vmem, sems,
):
    heads, n_picks = mine.shape[2] // HEAD_DIM, picks.shape[1]
    at, line = lax.axis_index("tm"), lax.axis_index("height")
    odd, line_odd = lax.rem(at, 2), lax.rem(line, 2)
    sources = (face_1.at[:, line_odd], face_2.at[:, 1 - line_odd], part, a, b, outer)
    buffers = (face_1_vmem, face_2_vmem, *(far_vmem.at[i] for i in range(2 * REACH)))
    stream = Stream(sources, buffers, sems)
    query, grad = mine.at[0], mine.at[1]
    face_1_ok = (line_odd == 1) | (line + 1 < n_height)
    face_2_ok = jnp.where(line_odd == 1, line + 1 < n_height, line > 0)
    slot_at = (2 - odd, 3 - 3 * odd, 3 * odd, 1 + odd)
    rows = [own.shape[1], face_1_vmem.shape[1], face_2_vmem.shape[1]] + [own.shape[1]] * n_picks
    spans = [pl.ds(sum(rows[:i]), count) for i, count in enumerate(rows)]
    left, right = pl.ds(0, HEAD_DIM), pl.ds(HEAD_DIM, HEAD_DIM)

    def chosen(e, p):
        slot = picks[e, p]
        target = at + slot - jnp.where(slot < REACH, REACH, REACH - 1)
        ok = (target >= 0) & (target < n_tm)
        for before in range(p):
            ok &= picks[e, before] != slot
        return ok

    def place(e, p):
        return sum(jnp.where(picks[e, p] == slot, i, 0) for i, slot in enumerate(slot_at))

    def blocks(e, which):
        cols = columns(e)
        far = [far_vmem[place(e, p), which, :, cols] for p in range(n_picks)]
        return [own[which, :, cols], face_1_vmem[which, :, cols], face_2_vmem[which, :, cols], *far]

    def products(e):
        stream.ready(e)
        both = corners(query[:, columns(e)], grad[:, columns(e)])
        for key, value, span in zip(blocks(e, 0), blocks(e, 1), spans):
            scratch[e % 2, span, :] = dot(jnp.concatenate([key, value], axis=1), both, NT)

    def softmax(e):
        present = [None, face_1_ok, face_2_ok] + [chosen(e, p) for p in range(n_picks)]
        score = [scratch.at[e % 2, span, left] for span in spans]
        grad_weight = [scratch.at[e % 2, span, right] for span in spans]
        tops = [jnp.max(s[...], axis=0, keepdims=True) for s in score]
        tops = [t if ok is None else jnp.where(ok, t, -jnp.inf) for t, ok in zip(tops, present)]
        top = functools.reduce(jnp.maximum, tops) * (SCALE * LOG2E)
        expo = [
            jnp.exp2(s[...] * (SCALE * LOG2E) - (top if ok is None else jnp.where(ok, top, FAR_AWAY)))
            for s, ok in zip(score, present)
        ]
        total = sum(jnp.sum(x, axis=0, keepdims=True) for x in expo)
        inverse = 1.0 / total
        delta = sum(jnp.sum(x * w[...], axis=0, keepdims=True) for x, w in zip(expo, grad_weight))
        delta, level = delta * inverse, top + jnp.log2(total)
        stats[0, e : e + 1, :] = delta
        for i, slot in enumerate(slot_at):
            ok = [present[3 + p] & (picks[e, p] == slot) for p in range(n_picks)]
            stats[1 + i, e : e + 1, :] = jnp.where(functools.reduce(jnp.logical_or, ok), level, FAR_AWAY)
        for i, (x, w, span) in enumerate(zip(expo, grad_weight, spans)):
            weights = x * inverse
            graded[e % 2, span, left] = (weights * (w[...] - delta) * SCALE).astype(jnp.bfloat16)
            if i < 3:
                graded[e % 2, span, right] = weights.astype(jnp.bfloat16)

    def gradients(e):
        cols = columns(e)
        dq = dot(graded[e % 2, :, left], jnp.concatenate(blocks(e, 0), axis=0), TN)
        grad_query[:, cols] = dq.astype(grad_query.dtype)
        both = corners(query[:, cols], grad[:, cols])
        for out, span in zip((own_grads, face_1_grads, face_2_grads), spans):
            grads = dot(graded[e % 2, span, :], both, NN)
            out[0, :, cols] = grads[:, :HEAD_DIM].astype(out.dtype)
            out[1, :, cols] = grads[:, HEAD_DIM:].astype(out.dtype)

    for step in range(heads + 2):
        if step < heads:
            products(step)
        if 0 <= step - 1 < heads:
            softmax(step - 1)
        if 0 <= step - 2:
            gradients(step - 2)


def key_kernel(
    keys, own_grads, face_1_grads, face_2_grads, part, a, b, outer, of_part, of_a, of_b,
    grad_key, grad_value, scratch,
):
    heads, face = keys.shape[2] // HEAD_DIM, face_1_grads.shape[1]
    last_first = lax.rem(lax.axis_index("height"), 2) == 0
    others = ((part, of_part.at[0], 1), (a, of_a, 3), (b, of_b, 2), (outer, of_part.at[1], 4))

    def products(e):
        cols = columns(e)
        pair = jnp.concatenate([keys[0, :, cols], keys[1, :, cols]], axis=1)
        for i, (block, _, _) in enumerate(others):
            scratch[e % 2, i] = dot(pair, corners(block[0, :, cols], block[1, :, cols]), NT)

    def finish(e):
        cols = columns(e)
        sums = jnp.concatenate([own_grads[0, :, cols], own_grads[1, :, cols]], axis=1)
        for i, (block, stats, slot) in enumerate(others):
            score, grad_weights = scratch[e % 2, i, :, :HEAD_DIM], scratch[e % 2, i, :, HEAD_DIM:]
            weights = jnp.exp2(score * (SCALE * LOG2E) - stats[slot, e : e + 1, :])
            dscore = weights * (grad_weights - stats[0, e : e + 1, :]) * SCALE
            both = jnp.concatenate([dscore.astype(jnp.bfloat16), weights.astype(jnp.bfloat16)], axis=1)
            sums += dot(both, corners(block[0, :, cols], block[1, :, cols]), NN)
        for at, out in ((0, grad_key), (1, grad_value)):
            one = face_1_grads[at, :, cols].astype(jnp.float32)
            two = face_2_grads[at, :, cols].astype(jnp.float32)
            first, last = jnp.where(last_first, two, one), jnp.where(last_first, one, two)
            part_sum = sums[:, at * HEAD_DIM : (at + 1) * HEAD_DIM]
            out[:face, cols] = (part_sum[:face] + first).astype(out.dtype)
            out[face:, cols] = (part_sum[face:] + last).astype(out.dtype)

    products(0)
    for e in range(heads):
        if e + 1 < heads:
            products(e + 1)
        finish(e)


def per_device(query_tok, key_tok, value_tok, grad_out, far_picks):
    frames_dev, rows_dev, columns, width = query_tok.shape
    tile, face = frames_dev * rows_dev * columns, frames_dev * columns
    heads, n_picks = width // HEAD_DIM, far_picks.shape[3]
    n_tm, n_height = lax.axis_size("tm"), lax.axis_size("height")
    query, key = query_tok.reshape(tile, width), key_tok.reshape(tile, width)
    value, grad = value_tok.reshape(tile, width), grad_out.reshape(tile, width)
    partner, route_a, route_b, outer = routes(n_tm)
    relayed = n_tm % 2 == 0
    pairs_1 = [(i, i ^ 1) for i in range(n_height) if i ^ 1 < n_height]
    pairs_2 = [(i, i - 1 if i % 2 == 0 else i + 1) for i in range(n_height)]
    pairs_2 = [(i, j) for i, j in pairs_2 if 0 <= j < n_height]

    def move(block, route):
        return lax.ppermute(block, "tm", route)

    key_value, query_grad = paired(key, value, query, grad)
    kv_part, kv_b = move(key_value, partner), move(key_value, route_b)
    kv_a = move(after(key_value, kv_part), route_a)
    face_1 = lax.ppermute(key_value, "height", pairs_1)
    qg_part = move(after(query_grad, kv_part), partner)
    qg_a = move(query_grad, route_a)
    kv_outer = move(after(kv_part, face_1), route_b) if relayed else move(key_value, outer)
    qg_b = move(after(query_grad, kv_b), route_b)
    face_2 = lax.ppermute(after(key_value, qg_a), "height", pairs_2)
    qg_outer = move(qg_a, partner) if relayed else move(query_grad, outer)

    f32, bf16 = jnp.float32, jnp.bfloat16
    vmem, hbm = pl.BlockSpec(memory_space=pltpu.VMEM), pl.BlockSpec(memory_space=pltpu.HBM)
    block = 2 * tile * tile * HEAD_DIM * heads
    params = pltpu.CompilerParams(vmem_limit_bytes=VMEM_BYTES)
    by_row = (2, rows_dev, face, width)
    grad_query, own_grads, face_1_grads, face_2_grads, stats = pl.pallas_call(
        functools.partial(query_kernel, n_tm, n_height),
        out_shape=(
            jax.ShapeDtypeStruct((tile, width), bf16),
            jax.ShapeDtypeStruct((2, tile, width), f32),
            jax.ShapeDtypeStruct((2, face, width), bf16),
            jax.ShapeDtypeStruct((2, face, width), bf16),
            jax.ShapeDtypeStruct((1 + 2 * REACH, heads, tile), f32),
        ),
        in_specs=[vmem] * 2 + [hbm] * 6 + [pl.BlockSpec(memory_space=pltpu.SMEM)],
        out_specs=[vmem] * 5,
        scratch_shapes=[
            pltpu.VMEM((2, tile * (1 + n_picks) + 2 * face, 2 * HEAD_DIM), f32),
            pltpu.VMEM((2, tile * (1 + n_picks) + 2 * face, 2 * HEAD_DIM), bf16),
            *[pltpu.VMEM((2, face, width), bf16)] * 2,
            pltpu.VMEM((2 * REACH, 2, tile, width), bf16),
            stream_sems(heads, 2 + 2 * REACH),
        ],
        compiler_params=params,
        cost_estimate=pl.CostEstimate(flops=200 * block, bytes_accessed=4 << 20, transcendentals=0),
        name="query_side",
    )(query_grad, key_value, in_hbm(face_1.reshape(by_row)), in_hbm(face_2.reshape(by_row)),
      in_hbm(kv_part), in_hbm(kv_a), in_hbm(kv_b), in_hbm(kv_outer),
      far_picks.reshape(heads, n_picks))

    of_a, of_b = move(stats, route_a), move(stats, route_b)
    of_part = move(jnp.stack([stats, of_a]), partner)
    if not relayed:
        of_part = jnp.stack([of_part[0], move(stats, outer)])
    back_1 = lax.ppermute(face_1_grads, "height", pairs_1)
    back_2 = lax.ppermute(face_2_grads, "height", pairs_2)

    grad_key, grad_value = pl.pallas_call(
        key_kernel,
        out_shape=(jax.ShapeDtypeStruct((tile, width), bf16),) * 2,
        in_specs=[vmem] * 11,
        out_specs=[vmem] * 2,
        scratch_shapes=[pltpu.VMEM((2, 2 * REACH, tile, 2 * HEAD_DIM), f32)],
        compiler_params=params,
        cost_estimate=pl.CostEstimate(flops=100 * block, bytes_accessed=4 << 20, transcendentals=0),
        name="key_side",
    )(key_value, own_grads, back_1, back_2, qg_part, qg_a, qg_b, qg_outer, of_part, of_a, of_b)
    return tuple(x.reshape(query_tok.shape) for x in (grad_query, grad_key, grad_value))


def solution(mesh):
    spec = P("tm", "height", None, None)
    return jax.shard_map(
        per_device, mesh=mesh, in_specs=(spec,) * 5, out_specs=(spec,) * 3, check_vma=False
    )
```

```python
import functools

import jax
import jax.numpy as jnp
from jax import lax
from jax.experimental import pallas as pl
from jax.experimental.pallas import tpu as pltpu
from jax.sharding import PartitionSpec as P

HEAD_DIM = 128
REACH = 2
SCALE = HEAD_DIM**-0.5
LOG2E = 1.4426950408889634
FAR_AWAY = 3e38
VMEM_BYTES = 12 * 1024 * 1024
NT = (((1,), (1,)), ((), ()))
NN = (((1,), (0,)), ((), ()))
TN = (((0,), (0,)), ((), ()))


def dot(left, right, dims):
    return lax.dot_general(left, right, dims, preferred_element_type=jnp.float32)


def corners(first, second):
    zero = jnp.zeros_like(first)
    top = jnp.concatenate([first, zero], axis=1)
    return jnp.concatenate([top, jnp.concatenate([zero, second], axis=1)], axis=0)


def columns(e):
    return pl.ds(e * HEAD_DIM, HEAD_DIM)


def routes(size):
    def keep(move):
        return [(i, move(i)) for i in range(size) if 0 <= move(i) < size]

    partner = keep(lambda i: i ^ 1)
    route_a = keep(lambda i: i - 2 if i % 2 == 0 else i + 2)
    route_b = keep(lambda i: i + 2 if i % 2 == 0 else i - 2)
    outer = keep(lambda i: i - 1 if i % 2 == 0 else i + 1)
    return partner, route_a, route_b, outer


def after(value, *done):
    return lax.optimization_barrier((value, *done))[0]


def in_hbm(block):
    return pltpu.with_memory_space_constraint(block, pltpu.HBM)


def pair_kernel(key, value, query, grad, key_value, query_grad, sems):
    parts = sems.shape[1]
    rows = key.shape[0] // parts
    copies = []
    for i, (source, out) in enumerate(
        ((key, key_value.at[0]), (value, key_value.at[1]), (query, query_grad.at[0]), (grad, query_grad.at[1]))
    ):
        for part in range(parts):
            at = pl.ds(part * rows, rows)
            copies.append(pltpu.make_async_copy(source.at[at], out.at[at], sems.at[i, part]))
    for copy in copies:
        copy.start()
    for copy in copies:
        copy.wait()


def paired(*blocks):
    rows, width = blocks[0].shape
    parts = 4 if rows % 64 == 0 else 1
    return pl.pallas_call(
        pair_kernel,
        out_shape=(jax.ShapeDtypeStruct((2, rows, width), blocks[0].dtype),) * 2,
        in_specs=[pl.BlockSpec(memory_space=pltpu.HBM)] * 4,
        out_specs=[pl.BlockSpec(memory_space=pltpu.VMEM)] * 2,
        scratch_shapes=[pltpu.SemaphoreType.DMA((4, parts))],
        compiler_params=pltpu.CompilerParams(vmem_limit_bytes=VMEM_BYTES),
        cost_estimate=pl.CostEstimate(flops=0, bytes_accessed=16 * rows * width, transcendentals=0),
        name="pairs",
    )(*map(in_hbm, blocks))


class Stream:
    def __init__(self, sources, buffers, sems):
        heads = buffers[0].shape[2] // HEAD_DIM
        self.starts = stream_starts(heads)
        self.ends = self.starts[1:] + [heads]
        self.sources, self.buffers, self.sems = sources, buffers, sems
        for chunk in range(len(self.starts)):
            for i in range(len(sources)):
                self.copy(chunk, i).start()

    def copy(self, chunk, i):
        cols = pl.ds(self.starts[chunk] * HEAD_DIM, (self.ends[chunk] - self.starts[chunk]) * HEAD_DIM)
        return pltpu.make_async_copy(
            self.sources[i].at[:, :, cols], self.buffers[i].at[:, :, cols], self.sems.at[chunk, i]
        )

    def ready(self, e):
        if e in self.starts:
            for i in range(len(self.sources)):
                self.copy(self.starts.index(e), i).wait()


def stream_starts(heads):
    return [at for at in (0, 1, 3, 7) if at < heads]


def stream_sems(heads, count):
    return pltpu.SemaphoreType.DMA((len(stream_starts(heads)), count))


def query_kernel(
    n_tm, n_height, mine, own, face_1, face_2, part, a, b, outer, picks,
    grad_query, own_grads, face_1_grads, face_2_grads, stats,
    scratch, graded, face_1_vmem, face_2_vmem, far_vmem, sems,
):
    heads, n_picks = mine.shape[2] // HEAD_DIM, picks.shape[1]
    at, line = lax.axis_index("tm"), lax.axis_index("height")
    odd, line_odd = lax.rem(at, 2), lax.rem(line, 2)
    sources = (face_1.at[:, line_odd], face_2.at[:, 1 - line_odd], part, a, b, outer)
    buffers = (face_1_vmem, face_2_vmem, *(far_vmem.at[i] for i in range(2 * REACH)))
    stream = Stream(sources, buffers, sems)
    query, grad = mine.at[0], mine.at[1]
    face_1_ok = (line_odd == 1) | (line + 1 < n_height)
    face_2_ok = jnp.where(line_odd == 1, line + 1 < n_height, line > 0)
    slot_at = (2 - odd, 3 - 3 * odd, 3 * odd, 1 + odd)
    rows = [own.shape[1], face_1_vmem.shape[1], face_2_vmem.shape[1]] + [own.shape[1]] * n_picks
    spans = [pl.ds(sum(rows[:i]), count) for i, count in enumerate(rows)]
    left, right = pl.ds(0, HEAD_DIM), pl.ds(HEAD_DIM, HEAD_DIM)

    def chosen(e, p):
        slot = picks[e, p]
        target = at + slot - jnp.where(slot < REACH, REACH, REACH - 1)
        ok = (target >= 0) & (target < n_tm)
        for before in range(p):
            ok &= picks[e, before] != slot
        return ok

    def place(e, p):
        return sum(jnp.where(picks[e, p] == slot, i, 0) for i, slot in enumerate(slot_at))

    def blocks(e, which):
        cols = columns(e)
        far = [far_vmem[place(e, p), which, :, cols] for p in range(n_picks)]
        return [own[which, :, cols], face_1_vmem[which, :, cols], face_2_vmem[which, :, cols], *far]

    def products(e):
        stream.ready(e)
        both = corners(query[:, columns(e)], grad[:, columns(e)])
        for key, value, span in zip(blocks(e, 0), blocks(e, 1), spans):
            scratch[e % 2, span, :] = dot(jnp.concatenate([key, value], axis=1), both, NT)

    def softmax(e):
        present = [None, face_1_ok, face_2_ok] + [chosen(e, p) for p in range(n_picks)]
        score = [scratch.at[e % 2, span, left] for span in spans]
        grad_weight = [scratch.at[e % 2, span, right] for span in spans]
        tops = [jnp.max(s[...], axis=0, keepdims=True) for s in score]
        tops = [t if ok is None else jnp.where(ok, t, -jnp.inf) for t, ok in zip(tops, present)]
        top = functools.reduce(jnp.maximum, tops) * (SCALE * LOG2E)
        expo = [
            jnp.exp2(s[...] * (SCALE * LOG2E) - (top if ok is None else jnp.where(ok, top, FAR_AWAY)))
            for s, ok in zip(score, present)
        ]
        total = sum(jnp.sum(x, axis=0, keepdims=True) for x in expo)
        inverse = 1.0 / total
        delta = sum(jnp.sum(x * w[...], axis=0, keepdims=True) for x, w in zip(expo, grad_weight))
        delta, level = delta * inverse, top + jnp.log2(total)
        stats[0, e : e + 1, :] = delta
        for i, slot in enumerate(slot_at):
            ok = [present[3 + p] & (picks[e, p] == slot) for p in range(n_picks)]
            stats[1 + i, e : e + 1, :] = jnp.where(functools.reduce(jnp.logical_or, ok), level, FAR_AWAY)
        for i, (x, w, span) in enumerate(zip(expo, grad_weight, spans)):
            weights = x * inverse
            graded[e % 2, span, left] = (weights * (w[...] - delta) * SCALE).astype(jnp.bfloat16)
            if i < 3:
                graded[e % 2, span, right] = weights.astype(jnp.bfloat16)

    def gradients(e):
        cols = columns(e)
        dq = dot(graded[e % 2, :, left], jnp.concatenate(blocks(e, 0), axis=0), TN)
        grad_query[:, cols] = dq.astype(grad_query.dtype)
        both = corners(query[:, cols], grad[:, cols])
        for out, span in zip((own_grads, face_1_grads, face_2_grads), spans):
            grads = dot(graded[e % 2, span, :], both, NN)
            out[0, :, cols] = grads[:, :HEAD_DIM].astype(out.dtype)
            out[1, :, cols] = grads[:, HEAD_DIM:].astype(out.dtype)

    for step in range(heads + 2):
        if step < heads:
            products(step)
        if 0 <= step - 1 < heads:
            softmax(step - 1)
        if 0 <= step - 2:
            gradients(step - 2)


def key_kernel(
    keys, own_grads, face_1_grads, face_2_grads, part, a, b, outer, of_part, of_a, of_b,
    grad_key, grad_value, scratch,
):
    heads, face = keys.shape[2] // HEAD_DIM, face_1_grads.shape[1]
    last_first = lax.rem(lax.axis_index("height"), 2) == 0
    others = ((part, of_part.at[0], 1), (a, of_a, 3), (b, of_b, 2), (outer, of_part.at[1], 4))

    def products(e):
        cols = columns(e)
        pair = jnp.concatenate([keys[0, :, cols], keys[1, :, cols]], axis=1)
        for i, (block, _, _) in enumerate(others):
            scratch[e % 2, i] = dot(pair, corners(block[0, :, cols], block[1, :, cols]), NT)

    def finish(e):
        cols = columns(e)
        sums = jnp.concatenate([own_grads[0, :, cols], own_grads[1, :, cols]], axis=1)
        for i, (block, stats, slot) in enumerate(others):
            score, grad_weights = scratch[e % 2, i, :, :HEAD_DIM], scratch[e % 2, i, :, HEAD_DIM:]
            weights = jnp.exp2(score * (SCALE * LOG2E) - stats[slot, e : e + 1, :])
            dscore = weights * (grad_weights - stats[0, e : e + 1, :]) * SCALE
            both = jnp.concatenate([dscore.astype(jnp.bfloat16), weights.astype(jnp.bfloat16)], axis=1)
            sums += dot(both, corners(block[0, :, cols], block[1, :, cols]), NN)
        for at, out in ((0, grad_key), (1, grad_value)):
            one = face_1_grads[at, :, cols].astype(jnp.float32)
            two = face_2_grads[at, :, cols].astype(jnp.float32)
            first, last = jnp.where(last_first, two, one), jnp.where(last_first, one, two)
            part_sum = sums[:, at * HEAD_DIM : (at + 1) * HEAD_DIM]
            out[:face, cols] = (part_sum[:face] + first).astype(out.dtype)
            out[face:, cols] = (part_sum[face:] + last).astype(out.dtype)

    products(0)
    for e in range(heads):
        if e + 1 < heads:
            products(e + 1)
        finish(e)


def per_device(query_tok, key_tok, value_tok, grad_out, far_picks):
    frames_dev, rows_dev, columns, width = query_tok.shape
    tile, face = frames_dev * rows_dev * columns, frames_dev * columns
    heads, n_picks = width // HEAD_DIM, far_picks.shape[3]
    n_tm, n_height = lax.axis_size("tm"), lax.axis_size("height")
    query, key = query_tok.reshape(tile, width), key_tok.reshape(tile, width)
    value, grad = value_tok.reshape(tile, width), grad_out.reshape(tile, width)
    partner, route_a, route_b, outer = routes(n_tm)
    relayed = n_tm % 2 == 0
    pairs_1 = [(i, i ^ 1) for i in range(n_height) if i ^ 1 < n_height]
    pairs_2 = [(i, i - 1 if i % 2 == 0 else i + 1) for i in range(n_height)]
    pairs_2 = [(i, j) for i, j in pairs_2 if 0 <= j < n_height]

    def move(block, route):
        return lax.ppermute(block, "tm", route)

    key_value, query_grad = paired(key, value, query, grad)
    kv_part, kv_b = move(key_value, partner), move(key_value, route_b)
    kv_a = move(after(key_value, kv_part), route_a)
    face_1 = lax.ppermute(key_value, "height", pairs_1)
    qg_part = move(query_grad, partner)
    qg_a = move(query_grad, route_a)
    kv_outer = move(after(kv_part, face_1), route_b) if relayed else move(key_value, outer)
    qg_b = move(after(query_grad, kv_b), route_b)
    face_2 = lax.ppermute(after(key_value, qg_a), "height", pairs_2)
    qg_outer = move(after(qg_a, qg_part), partner) if relayed else move(query_grad, outer)

    f32, bf16 = jnp.float32, jnp.bfloat16
    vmem, hbm = pl.BlockSpec(memory_space=pltpu.VMEM), pl.BlockSpec(memory_space=pltpu.HBM)
    block = 2 * tile * tile * HEAD_DIM * heads
    params = pltpu.CompilerParams(vmem_limit_bytes=VMEM_BYTES)
    by_row = (2, rows_dev, face, width)
    grad_query, own_grads, face_1_grads, face_2_grads, stats = pl.pallas_call(
        functools.partial(query_kernel, n_tm, n_height),
        out_shape=(
            jax.ShapeDtypeStruct((tile, width), bf16),
            jax.ShapeDtypeStruct((2, tile, width), f32),
            jax.ShapeDtypeStruct((2, face, width), bf16),
            jax.ShapeDtypeStruct((2, face, width), bf16),
            jax.ShapeDtypeStruct((1 + 2 * REACH, heads, tile), f32),
        ),
        in_specs=[vmem] * 2 + [hbm] * 6 + [pl.BlockSpec(memory_space=pltpu.SMEM)],
        out_specs=[vmem] * 5,
        scratch_shapes=[
            pltpu.VMEM((2, tile * (1 + n_picks) + 2 * face, 2 * HEAD_DIM), f32),
            pltpu.VMEM((2, tile * (1 + n_picks) + 2 * face, 2 * HEAD_DIM), bf16),
            *[pltpu.VMEM((2, face, width), bf16)] * 2,
            pltpu.VMEM((2 * REACH, 2, tile, width), bf16),
            stream_sems(heads, 2 + 2 * REACH),
        ],
        compiler_params=params,
        cost_estimate=pl.CostEstimate(flops=200 * block, bytes_accessed=4 << 20, transcendentals=0),
        name="query_side",
    )(query_grad, key_value, in_hbm(face_1.reshape(by_row)), in_hbm(face_2.reshape(by_row)),
      in_hbm(kv_part), in_hbm(kv_a), in_hbm(kv_b), in_hbm(kv_outer),
      far_picks.reshape(heads, n_picks))

    of_a, of_b = move(stats, route_a), move(stats, route_b)
    of_part = move(jnp.stack([stats, of_a]), partner)
    if not relayed:
        of_part = jnp.stack([of_part[0], move(stats, outer)])
    back_1 = lax.ppermute(face_1_grads, "height", pairs_1)
    back_2 = lax.ppermute(face_2_grads, "height", pairs_2)

    grad_key, grad_value = pl.pallas_call(
        key_kernel,
        out_shape=(jax.ShapeDtypeStruct((tile, width), bf16),) * 2,
        in_specs=[vmem] * 11,
        out_specs=[vmem] * 2,
        scratch_shapes=[pltpu.VMEM((2, 2 * REACH, tile, 2 * HEAD_DIM), f32)],
        compiler_params=params,
        cost_estimate=pl.CostEstimate(flops=100 * block, bytes_accessed=4 << 20, transcendentals=0),
        name="key_side",
    )(key_value, own_grads, back_1, back_2, qg_part, qg_a, qg_b, qg_outer, of_part, of_a, of_b)
    return tuple(x.reshape(query_tok.shape) for x in (grad_query, grad_key, grad_value))


def solution(mesh):
    spec = P("tm", "height", None, None)
    return jax.shard_map(
        per_device, mesh=mesh, in_specs=(spec,) * 5, out_specs=(spec,) * 3, check_vma=False
    )
```

```python
import functools

import jax
import jax.numpy as jnp
from jax import lax
from jax.experimental import pallas as pl
from jax.experimental.pallas import tpu as pltpu
from jax.sharding import PartitionSpec as P

HEAD_DIM = 128
REACH = 2
SCALE = HEAD_DIM**-0.5
LOG2E = 1.4426950408889634
FAR_AWAY = 3e38
VMEM_BYTES = 12 * 1024 * 1024
NT = (((1,), (1,)), ((), ()))
NN = (((1,), (0,)), ((), ()))
TN = (((0,), (0,)), ((), ()))


def dot(left, right, dims):
    return lax.dot_general(left, right, dims, preferred_element_type=jnp.float32)


def corners(first, second):
    zero = jnp.zeros_like(first)
    top = jnp.concatenate([first, zero], axis=1)
    return jnp.concatenate([top, jnp.concatenate([zero, second], axis=1)], axis=0)


def columns(e):
    return pl.ds(e * HEAD_DIM, HEAD_DIM)


def routes(size):
    def keep(move):
        return [(i, move(i)) for i in range(size) if 0 <= move(i) < size]

    partner = keep(lambda i: i ^ 1)
    route_a = keep(lambda i: i - 2 if i % 2 == 0 else i + 2)
    route_b = keep(lambda i: i + 2 if i % 2 == 0 else i - 2)
    outer = keep(lambda i: i - 1 if i % 2 == 0 else i + 1)
    return partner, route_a, route_b, outer


def after(value, *done):
    return lax.optimization_barrier((value, *done))[0]


def in_hbm(block):
    return pltpu.with_memory_space_constraint(block, pltpu.HBM)


def pair_kernel(key, value, query, grad, key_value, query_grad, sems):
    parts = sems.shape[1]
    rows = key.shape[0] // parts
    copies = []
    for i, (source, out) in enumerate(
        ((key, key_value.at[0]), (value, key_value.at[1]), (query, query_grad.at[0]), (grad, query_grad.at[1]))
    ):
        for part in range(parts):
            at = pl.ds(part * rows, rows)
            copies.append(pltpu.make_async_copy(source.at[at], out.at[at], sems.at[i, part]))
    for copy in copies:
        copy.start()
    for copy in copies:
        copy.wait()


def paired(*blocks):
    rows, width = blocks[0].shape
    parts = 4 if rows % 64 == 0 else 1
    return pl.pallas_call(
        pair_kernel,
        out_shape=(jax.ShapeDtypeStruct((2, rows, width), blocks[0].dtype),) * 2,
        in_specs=[pl.BlockSpec(memory_space=pltpu.HBM)] * 4,
        out_specs=[pl.BlockSpec(memory_space=pltpu.VMEM)] * 2,
        scratch_shapes=[pltpu.SemaphoreType.DMA((4, parts))],
        compiler_params=pltpu.CompilerParams(vmem_limit_bytes=VMEM_BYTES),
        cost_estimate=pl.CostEstimate(flops=0, bytes_accessed=16 * rows * width, transcendentals=0),
        name="pairs",
    )(*map(in_hbm, blocks))


class Stream:
    def __init__(self, sources, buffers, sems):
        heads = buffers[0].shape[2] // HEAD_DIM
        self.starts = stream_starts(heads)
        self.ends = self.starts[1:] + [heads]
        self.sources, self.buffers, self.sems = sources, buffers, sems
        for chunk in range(len(self.starts)):
            for i in range(len(sources)):
                self.copy(chunk, i).start()

    def copy(self, chunk, i):
        cols = pl.ds(self.starts[chunk] * HEAD_DIM, (self.ends[chunk] - self.starts[chunk]) * HEAD_DIM)
        return pltpu.make_async_copy(
            self.sources[i].at[:, :, cols], self.buffers[i].at[:, :, cols], self.sems.at[chunk, i]
        )

    def ready(self, e):
        if e in self.starts:
            for i in range(len(self.sources)):
                self.copy(self.starts.index(e), i).wait()


def stream_starts(heads):
    return [at for at in (0, 1, 3, 7) if at < heads]


def stream_sems(heads, count):
    return pltpu.SemaphoreType.DMA((len(stream_starts(heads)), count))


def query_kernel(
    n_tm, n_height, mine, own, face_1, face_2, part, a, b, outer, picks,
    grad_query, own_grads, face_1_grads, face_2_grads, stats,
    scratch, graded, face_1_vmem, face_2_vmem, far_vmem, sems,
):
    heads, n_picks = mine.shape[2] // HEAD_DIM, picks.shape[1]
    at, line = lax.axis_index("tm"), lax.axis_index("height")
    odd, line_odd = lax.rem(at, 2), lax.rem(line, 2)
    sources = (face_1.at[:, line_odd], face_2.at[:, 1 - line_odd], part, a, b, outer)
    buffers = (face_1_vmem, face_2_vmem, *(far_vmem.at[i] for i in range(2 * REACH)))
    stream = Stream(sources, buffers, sems)
    query, grad = mine.at[0], mine.at[1]
    face_1_ok = (line_odd == 1) | (line + 1 < n_height)
    face_2_ok = jnp.where(line_odd == 1, line + 1 < n_height, line > 0)
    slot_at = (2 - odd, 3 - 3 * odd, 3 * odd, 1 + odd)
    rows = [own.shape[1], face_1_vmem.shape[1], face_2_vmem.shape[1]] + [own.shape[1]] * n_picks
    spans = [pl.ds(sum(rows[:i]), count) for i, count in enumerate(rows)]
    left, right = pl.ds(0, HEAD_DIM), pl.ds(HEAD_DIM, HEAD_DIM)

    def chosen(e, p):
        slot = picks[e, p]
        target = at + slot - jnp.where(slot < REACH, REACH, REACH - 1)
        ok = (target >= 0) & (target < n_tm)
        for before in range(p):
            ok &= picks[e, before] != slot
        return ok

    def place(e, p):
        return sum(jnp.where(picks[e, p] == slot, i, 0) for i, slot in enumerate(slot_at))

    def blocks(e, which):
        cols = columns(e)
        far = [far_vmem[place(e, p), which, :, cols] for p in range(n_picks)]
        return [own[which, :, cols], face_1_vmem[which, :, cols], face_2_vmem[which, :, cols], *far]

    def products(e):
        stream.ready(e)
        both = corners(query[:, columns(e)], grad[:, columns(e)])
        for key, value, span in zip(blocks(e, 0), blocks(e, 1), spans):
            scratch[e % 2, span, :] = dot(jnp.concatenate([key, value], axis=1), both, NT)

    def softmax(e):
        present = [None, face_1_ok, face_2_ok] + [chosen(e, p) for p in range(n_picks)]
        score = [scratch.at[e % 2, span, left] for span in spans]
        grad_weight = [scratch.at[e % 2, span, right] for span in spans]
        tops = [jnp.max(s[...], axis=0, keepdims=True) for s in score]
        tops = [t if ok is None else jnp.where(ok, t, -jnp.inf) for t, ok in zip(tops, present)]
        top = functools.reduce(jnp.maximum, tops) * (SCALE * LOG2E)
        expo = [
            jnp.exp2(s[...] * (SCALE * LOG2E) - (top if ok is None else jnp.where(ok, top, FAR_AWAY)))
            for s, ok in zip(score, present)
        ]
        total = sum(jnp.sum(x, axis=0, keepdims=True) for x in expo)
        inverse = 1.0 / total
        delta = sum(jnp.sum(x * w[...], axis=0, keepdims=True) for x, w in zip(expo, grad_weight))
        delta, level = delta * inverse, top + jnp.log2(total)
        stats[0, e : e + 1, :] = delta
        for i, slot in enumerate(slot_at):
            ok = [present[3 + p] & (picks[e, p] == slot) for p in range(n_picks)]
            stats[1 + i, e : e + 1, :] = jnp.where(functools.reduce(jnp.logical_or, ok), level, FAR_AWAY)
        for i, (x, w, span) in enumerate(zip(expo, grad_weight, spans)):
            weights = x * inverse
            graded[e % 2, span, left] = (weights * (w[...] - delta) * SCALE).astype(jnp.bfloat16)
            if i < 3:
                graded[e % 2, span, right] = weights.astype(jnp.bfloat16)

    def gradients(e):
        cols = columns(e)
        dq = dot(graded[e % 2, :, left], jnp.concatenate(blocks(e, 0), axis=0), TN)
        grad_query[:, cols] = dq.astype(grad_query.dtype)
        both = corners(query[:, cols], grad[:, cols])
        for out, span in zip((own_grads, face_1_grads, face_2_grads), spans):
            grads = dot(graded[e % 2, span, :], both, NN)
            out[0, :, cols] = grads[:, :HEAD_DIM].astype(out.dtype)
            out[1, :, cols] = grads[:, HEAD_DIM:].astype(out.dtype)

    for step in range(heads + 2):
        if step < heads:
            products(step)
        if 0 <= step - 1 < heads:
            softmax(step - 1)
        if 0 <= step - 2:
            gradients(step - 2)


def far_grads(keys, others, sums, store, scratch):
    heads = keys.shape[2] // HEAD_DIM

    def products(e):
        cols = columns(e)
        pair = jnp.concatenate([keys[0, :, cols], keys[1, :, cols]], axis=1)
        for i, (block, _, _) in enumerate(others):
            scratch[e % 2, i] = dot(pair, corners(block[0, :, cols], block[1, :, cols]), NT)

    def finish(e):
        cols = columns(e)
        total = jnp.concatenate([sums[0, :, cols], sums[1, :, cols]], axis=1)
        for i, (block, stats, slot) in enumerate(others):
            score, grad_weights = scratch[e % 2, i, :, :HEAD_DIM], scratch[e % 2, i, :, HEAD_DIM:]
            weights = jnp.exp2(score * (SCALE * LOG2E) - stats[slot, e : e + 1, :])
            dscore = weights * (grad_weights - stats[0, e : e + 1, :]) * SCALE
            both = jnp.concatenate([dscore.astype(jnp.bfloat16), weights.astype(jnp.bfloat16)], axis=1)
            total += dot(both, corners(block[0, :, cols], block[1, :, cols]), NN)
        store(cols, total)

    products(0)
    for e in range(heads):
        if e + 1 < heads:
            products(e + 1)
        finish(e)


def key_kernel(
    keys, own_grads, face_1_grads, face_2_grads, part, b, outer, of_part, of_b, sums_out, scratch
):
    face = face_1_grads.shape[1]
    last_first = lax.rem(lax.axis_index("height"), 2) == 0

    def store(cols, total):
        for at in range(2):
            one = face_1_grads[at, :, cols].astype(jnp.float32)
            two = face_2_grads[at, :, cols].astype(jnp.float32)
            first, last = jnp.where(last_first, two, one), jnp.where(last_first, one, two)
            part_sum = total[:, at * HEAD_DIM : (at + 1) * HEAD_DIM]
            sums_out[at, :face, cols] = part_sum[:face] + first
            sums_out[at, face:, cols] = part_sum[face:] + last

    others = ((part, of_part, 1), (b, of_b.at[0], 2), (outer, of_b.at[1], 4))
    far_grads(keys, others, own_grads, store, scratch)


def last_kernel(keys, sums, a, of_a, grad_key, grad_value, scratch):
    def store(cols, total):
        grad_key[:, cols] = total[:, :HEAD_DIM].astype(grad_key.dtype)
        grad_value[:, cols] = total[:, HEAD_DIM:].astype(grad_value.dtype)

    far_grads(keys, ((a, of_a, 3),), sums, store, scratch)


def per_device(query_tok, key_tok, value_tok, grad_out, far_picks):
    frames_dev, rows_dev, columns, width = query_tok.shape
    tile, face = frames_dev * rows_dev * columns, frames_dev * columns
    heads, n_picks = width // HEAD_DIM, far_picks.shape[3]
    n_tm, n_height = lax.axis_size("tm"), lax.axis_size("height")
    query, key = query_tok.reshape(tile, width), key_tok.reshape(tile, width)
    value, grad = value_tok.reshape(tile, width), grad_out.reshape(tile, width)
    partner, route_a, route_b, outer = routes(n_tm)
    relayed = n_tm % 2 == 0
    pairs_1 = [(i, i ^ 1) for i in range(n_height) if i ^ 1 < n_height]
    pairs_2 = [(i, i - 1 if i % 2 == 0 else i + 1) for i in range(n_height)]
    pairs_2 = [(i, j) for i, j in pairs_2 if 0 <= j < n_height]

    def move(block, route):
        return lax.ppermute(block, "tm", route)

    key_value, query_grad = paired(key, value, query, grad)
    kv_part, kv_b = move(key_value, partner), move(key_value, route_b)
    kv_a = move(after(key_value, kv_part), route_a)
    face_1 = lax.ppermute(key_value, "height", pairs_1)
    qg_part = move(query_grad, partner)
    qg_a = move(query_grad, route_a)
    kv_outer = move(after(kv_part, face_1), route_b) if relayed else move(key_value, outer)
    qg_b = move(after(query_grad, kv_b), route_b)
    face_2 = lax.ppermute(after(key_value, qg_a), "height", pairs_2)
    qg_outer = move(after(qg_a, qg_part), partner) if relayed else move(query_grad, outer)

    f32, bf16 = jnp.float32, jnp.bfloat16
    vmem, hbm = pl.BlockSpec(memory_space=pltpu.VMEM), pl.BlockSpec(memory_space=pltpu.HBM)
    block = 2 * tile * tile * HEAD_DIM * heads
    params = pltpu.CompilerParams(vmem_limit_bytes=VMEM_BYTES)
    by_row = (2, rows_dev, face, width)
    grad_query, own_grads, face_1_grads, face_2_grads, stats = pl.pallas_call(
        functools.partial(query_kernel, n_tm, n_height),
        out_shape=(
            jax.ShapeDtypeStruct((tile, width), bf16),
            jax.ShapeDtypeStruct((2, tile, width), f32),
            jax.ShapeDtypeStruct((2, face, width), bf16),
            jax.ShapeDtypeStruct((2, face, width), bf16),
            jax.ShapeDtypeStruct((1 + 2 * REACH, heads, tile), f32),
        ),
        in_specs=[vmem] * 2 + [hbm] * 6 + [pl.BlockSpec(memory_space=pltpu.SMEM)],
        out_specs=[vmem] * 5,
        scratch_shapes=[
            pltpu.VMEM((2, tile * (1 + n_picks) + 2 * face, 2 * HEAD_DIM), f32),
            pltpu.VMEM((2, tile * (1 + n_picks) + 2 * face, 2 * HEAD_DIM), bf16),
            *[pltpu.VMEM((2, face, width), bf16)] * 2,
            pltpu.VMEM((2 * REACH, 2, tile, width), bf16),
            stream_sems(heads, 2 + 2 * REACH),
        ],
        compiler_params=params,
        cost_estimate=pl.CostEstimate(flops=200 * block, bytes_accessed=4 << 20, transcendentals=0),
        name="query_side",
    )(query_grad, key_value, in_hbm(face_1.reshape(by_row)), in_hbm(face_2.reshape(by_row)),
      in_hbm(kv_part), in_hbm(kv_a), in_hbm(kv_b), in_hbm(kv_outer),
      far_picks.reshape(heads, n_picks))

    of_part, of_a = move(stats, partner), move(stats, route_a)
    of_b = move(jnp.stack([stats, of_part]), route_b)
    if not relayed:
        of_b = jnp.stack([of_b[0], move(stats, outer)])
    back_1 = lax.ppermute(face_1_grads, "height", pairs_1)
    back_2 = lax.ppermute(face_2_grads, "height", pairs_2)

    sums = pl.pallas_call(
        key_kernel,
        out_shape=jax.ShapeDtypeStruct((2, tile, width), f32),
        in_specs=[vmem] * 9,
        out_specs=vmem,
        scratch_shapes=[pltpu.VMEM((2, 3, tile, 2 * HEAD_DIM), f32)],
        compiler_params=params,
        cost_estimate=pl.CostEstimate(flops=80 * block, bytes_accessed=4 << 20, transcendentals=0),
        name="key_side",
    )(key_value, own_grads, back_1, back_2, qg_part, qg_b, qg_outer, of_part, of_b)
    grad_key, grad_value = pl.pallas_call(
        last_kernel,
        out_shape=(jax.ShapeDtypeStruct((tile, width), bf16),) * 2,
        in_specs=[vmem] * 4,
        out_specs=[vmem] * 2,
        scratch_shapes=[pltpu.VMEM((2, 1, tile, 2 * HEAD_DIM), f32)],
        compiler_params=params,
        cost_estimate=pl.CostEstimate(flops=30 * block, bytes_accessed=4 << 20, transcendentals=0),
        name="last_side",
    )(key_value, sums, qg_a, of_a)
    return tuple(x.reshape(query_tok.shape) for x in (grad_query, grad_key, grad_value))


def solution(mesh):
    spec = P("tm", "height", None, None)
    return jax.shard_map(
        per_device, mesh=mesh, in_specs=(spec,) * 5, out_specs=(spec,) * 3, check_vma=False
    )
```

```python
import functools

import jax
import jax.numpy as jnp
from jax import lax
from jax.experimental import pallas as pl
from jax.experimental.pallas import tpu as pltpu
from jax.sharding import PartitionSpec as P

HEAD_DIM = 128
REACH = 2
SCALE = HEAD_DIM**-0.5
LOG2E = 1.4426950408889634
FAR_AWAY = 3e38
VMEM_BYTES = 12 * 1024 * 1024
NT = (((1,), (1,)), ((), ()))
NN = (((1,), (0,)), ((), ()))
TN = (((0,), (0,)), ((), ()))


def dot(left, right, dims):
    return lax.dot_general(left, right, dims, preferred_element_type=jnp.float32)


def corners(first, second):
    zero = jnp.zeros_like(first)
    top = jnp.concatenate([first, zero], axis=1)
    return jnp.concatenate([top, jnp.concatenate([zero, second], axis=1)], axis=0)


def columns(e):
    return pl.ds(e * HEAD_DIM, HEAD_DIM)


def routes(size):
    def keep(move):
        return [(i, move(i)) for i in range(size) if 0 <= move(i) < size]

    partner = keep(lambda i: i ^ 1)
    route_a = keep(lambda i: i - 2 if i % 2 == 0 else i + 2)
    route_b = keep(lambda i: i + 2 if i % 2 == 0 else i - 2)
    outer = keep(lambda i: i - 1 if i % 2 == 0 else i + 1)
    return partner, route_a, route_b, outer


def after(value, *done):
    return lax.optimization_barrier((value, *done))[0]


def in_hbm(block):
    return pltpu.with_memory_space_constraint(block, pltpu.HBM)


def pair_kernel(key, value, query, grad, key_value, query_grad, sems):
    parts = sems.shape[1]
    rows = key.shape[0] // parts
    copies = []
    for i, (source, out) in enumerate(
        ((key, key_value.at[0]), (value, key_value.at[1]), (query, query_grad.at[0]), (grad, query_grad.at[1]))
    ):
        for part in range(parts):
            at = pl.ds(part * rows, rows)
            copies.append(pltpu.make_async_copy(source.at[at], out.at[at], sems.at[i, part]))
    for copy in copies:
        copy.start()
    for copy in copies:
        copy.wait()


def paired(*blocks):
    rows, width = blocks[0].shape
    parts = 4 if rows % 64 == 0 else 1
    return pl.pallas_call(
        pair_kernel,
        out_shape=(jax.ShapeDtypeStruct((2, rows, width), blocks[0].dtype),) * 2,
        in_specs=[pl.BlockSpec(memory_space=pltpu.HBM)] * 4,
        out_specs=[pl.BlockSpec(memory_space=pltpu.VMEM)] * 2,
        scratch_shapes=[pltpu.SemaphoreType.DMA((4, parts))],
        compiler_params=pltpu.CompilerParams(vmem_limit_bytes=VMEM_BYTES),
        cost_estimate=pl.CostEstimate(flops=0, bytes_accessed=16 * rows * width, transcendentals=0),
        name="pairs",
    )(*map(in_hbm, blocks))


class Stream:
    def __init__(self, sources, buffers, sems):
        heads = buffers[0].shape[2] // HEAD_DIM
        self.starts = stream_starts(heads)
        self.ends = self.starts[1:] + [heads]
        self.sources, self.buffers, self.sems = sources, buffers, sems
        for chunk in range(len(self.starts)):
            for i in range(len(sources)):
                self.copy(chunk, i).start()

    def copy(self, chunk, i):
        cols = pl.ds(self.starts[chunk] * HEAD_DIM, (self.ends[chunk] - self.starts[chunk]) * HEAD_DIM)
        return pltpu.make_async_copy(
            self.sources[i].at[:, :, cols], self.buffers[i].at[:, :, cols], self.sems.at[chunk, i]
        )

    def ready(self, e):
        if e in self.starts:
            for i in range(len(self.sources)):
                self.copy(self.starts.index(e), i).wait()


def stream_starts(heads):
    return [at for at in (0, 1, 3, 7) if at < heads]


def stream_sems(heads, count):
    return pltpu.SemaphoreType.DMA((len(stream_starts(heads)), count))


def query_kernel(
    n_tm, n_height, mine, own, face_1, face_2, part, a, b, outer, picks,
    grad_query, own_grads, face_1_grads, face_2_grads, stats,
    scratch, graded, face_1_vmem, face_2_vmem, far_vmem, sems,
):
    heads, n_picks = mine.shape[2] // HEAD_DIM, picks.shape[1]
    at, line = lax.axis_index("tm"), lax.axis_index("height")
    odd, line_odd = lax.rem(at, 2), lax.rem(line, 2)
    sources = (face_1.at[:, line_odd], face_2.at[:, 1 - line_odd], part, a, b, outer)
    buffers = (face_1_vmem, face_2_vmem, *(far_vmem.at[i] for i in range(2 * REACH)))
    stream = Stream(sources, buffers, sems)
    query, grad = mine.at[0], mine.at[1]
    face_1_ok = (line_odd == 1) | (line + 1 < n_height)
    face_2_ok = jnp.where(line_odd == 1, line + 1 < n_height, line > 0)
    slot_at = (2 - odd, 3 - 3 * odd, 3 * odd, 1 + odd)
    rows = [own.shape[1], face_1_vmem.shape[1], face_2_vmem.shape[1]] + [own.shape[1]] * n_picks
    spans = [pl.ds(sum(rows[:i]), count) for i, count in enumerate(rows)]
    left, right = pl.ds(0, HEAD_DIM), pl.ds(HEAD_DIM, HEAD_DIM)

    def chosen(e, p):
        slot = picks[e, p]
        target = at + slot - jnp.where(slot < REACH, REACH, REACH - 1)
        ok = (target >= 0) & (target < n_tm)
        for before in range(p):
            ok &= picks[e, before] != slot
        return ok

    def place(e, p):
        return sum(jnp.where(picks[e, p] == slot, i, 0) for i, slot in enumerate(slot_at))

    def blocks(e, which):
        cols = columns(e)
        far = [far_vmem[place(e, p), which, :, cols] for p in range(n_picks)]
        return [own[which, :, cols], face_1_vmem[which, :, cols], face_2_vmem[which, :, cols], *far]

    def products(e):
        stream.ready(e)
        both = corners(query[:, columns(e)], grad[:, columns(e)])
        for key, value, span in zip(blocks(e, 0), blocks(e, 1), spans):
            scratch[e % 2, span, :] = dot(jnp.concatenate([key, value], axis=1), both, NT)

    def softmax(e):
        present = [None, face_1_ok, face_2_ok] + [chosen(e, p) for p in range(n_picks)]
        score = [scratch.at[e % 2, span, left] for span in spans]
        grad_weight = [scratch.at[e % 2, span, right] for span in spans]
        tops = [jnp.max(s[...], axis=0, keepdims=True) for s in score]
        tops = [t if ok is None else jnp.where(ok, t, -jnp.inf) for t, ok in zip(tops, present)]
        top = functools.reduce(jnp.maximum, tops) * (SCALE * LOG2E)
        expo = [
            jnp.exp2(s[...] * (SCALE * LOG2E) - (top if ok is None else jnp.where(ok, top, FAR_AWAY)))
            for s, ok in zip(score, present)
        ]
        total = sum(jnp.sum(x, axis=0, keepdims=True) for x in expo)
        inverse = 1.0 / total
        delta = sum(jnp.sum(x * w[...], axis=0, keepdims=True) for x, w in zip(expo, grad_weight))
        delta, level = delta * inverse, top + jnp.log2(total)
        stats[0, e : e + 1, :] = delta
        for i, slot in enumerate(slot_at):
            ok = [present[3 + p] & (picks[e, p] == slot) for p in range(n_picks)]
            stats[1 + i, e : e + 1, :] = jnp.where(functools.reduce(jnp.logical_or, ok), level, FAR_AWAY)
        for i, (x, w, span) in enumerate(zip(expo, grad_weight, spans)):
            weights = x * inverse
            graded[e % 2, span, left] = (weights * (w[...] - delta) * SCALE).astype(jnp.bfloat16)
            if i < 3:
                graded[e % 2, span, right] = weights.astype(jnp.bfloat16)

    def gradients(e):
        cols = columns(e)
        dq = dot(graded[e % 2, :, left], jnp.concatenate(blocks(e, 0), axis=0), TN)
        grad_query[:, cols] = dq.astype(grad_query.dtype)
        both = corners(query[:, cols], grad[:, cols])
        for out, span in zip((own_grads, face_1_grads, face_2_grads), spans):
            grads = dot(graded[e % 2, span, :], both, NN)
            out[0, :, cols] = grads[:, :HEAD_DIM].astype(out.dtype)
            out[1, :, cols] = grads[:, HEAD_DIM:].astype(out.dtype)

    for step in range(heads + 2):
        if step < heads:
            products(step)
        if 0 <= step - 1 < heads:
            softmax(step - 1)
        if 0 <= step - 2:
            gradients(step - 2)


def far_grads(keys, others, sums, store, scratch):
    heads, slots = keys.shape[2] // HEAD_DIM, scratch.shape[0]

    def products(e):
        cols = columns(e)
        pair = jnp.concatenate([keys[0, :, cols], keys[1, :, cols]], axis=1)
        for i, (block, _, _) in enumerate(others):
            scratch[e % slots, i] = dot(pair, corners(block[0, :, cols], block[1, :, cols]), NT)

    def finish(e):
        cols = columns(e)
        total = jnp.concatenate([sums[0, :, cols], sums[1, :, cols]], axis=1)
        for i, (block, stats, slot) in enumerate(others):
            score, grad_weights = scratch[e % slots, i, :, :HEAD_DIM], scratch[e % slots, i, :, HEAD_DIM:]
            weights = jnp.exp2(score * (SCALE * LOG2E) - stats[slot, e : e + 1, :])
            dscore = weights * (grad_weights - stats[0, e : e + 1, :]) * SCALE
            both = jnp.concatenate([dscore.astype(jnp.bfloat16), weights.astype(jnp.bfloat16)], axis=1)
            total += dot(both, corners(block[0, :, cols], block[1, :, cols]), NN)
        store(cols, total)

    for e in range(slots - 1):
        products(e)
    for e in range(heads):
        if e + slots - 1 < heads:
            products(e + slots - 1)
        finish(e)


def key_kernel(
    keys, own_grads, face_1_grads, face_2_grads, part, b, outer, of_part, of_b, sums_out, scratch
):
    face = face_1_grads.shape[1]
    last_first = lax.rem(lax.axis_index("height"), 2) == 0

    def store(cols, total):
        for at in range(2):
            one = face_1_grads[at, :, cols].astype(jnp.float32)
            two = face_2_grads[at, :, cols].astype(jnp.float32)
            first, last = jnp.where(last_first, two, one), jnp.where(last_first, one, two)
            part_sum = total[:, at * HEAD_DIM : (at + 1) * HEAD_DIM]
            sums_out[at, :face, cols] = part_sum[:face] + first
            sums_out[at, face:, cols] = part_sum[face:] + last

    others = ((part, of_part, 1), (b, of_b.at[0], 2), (outer, of_b.at[1], 4))
    far_grads(keys, others, own_grads, store, scratch)


def last_kernel(keys, sums, a, of_a, grad_key, grad_value, scratch):
    def store(cols, total):
        grad_key[:, cols] = total[:, :HEAD_DIM].astype(grad_key.dtype)
        grad_value[:, cols] = total[:, HEAD_DIM:].astype(grad_value.dtype)

    far_grads(keys, ((a, of_a, 3),), sums, store, scratch)


def per_device(query_tok, key_tok, value_tok, grad_out, far_picks):
    frames_dev, rows_dev, columns, width = query_tok.shape
    tile, face = frames_dev * rows_dev * columns, frames_dev * columns
    heads, n_picks = width // HEAD_DIM, far_picks.shape[3]
    n_tm, n_height = lax.axis_size("tm"), lax.axis_size("height")
    query, key = query_tok.reshape(tile, width), key_tok.reshape(tile, width)
    value, grad = value_tok.reshape(tile, width), grad_out.reshape(tile, width)
    partner, route_a, route_b, outer = routes(n_tm)
    relayed = n_tm % 2 == 0
    pairs_1 = [(i, i ^ 1) for i in range(n_height) if i ^ 1 < n_height]
    pairs_2 = [(i, i - 1 if i % 2 == 0 else i + 1) for i in range(n_height)]
    pairs_2 = [(i, j) for i, j in pairs_2 if 0 <= j < n_height]

    def move(block, route):
        return lax.ppermute(block, "tm", route)

    key_value, query_grad = paired(key, value, query, grad)
    kv_part, kv_b = move(key_value, partner), move(key_value, route_b)
    kv_a = move(after(key_value, kv_part), route_a)
    face_1 = lax.ppermute(key_value, "height", pairs_1)
    qg_part = move(query_grad, partner)
    qg_a = move(query_grad, route_a)
    kv_outer = move(after(kv_part, face_1), route_b) if relayed else move(key_value, outer)
    qg_b = move(after(query_grad, kv_b), route_b)
    face_2 = lax.ppermute(after(key_value, qg_a), "height", pairs_2)
    qg_outer = move(after(qg_a, qg_part), partner) if relayed else move(query_grad, outer)

    f32, bf16 = jnp.float32, jnp.bfloat16
    vmem, hbm = pl.BlockSpec(memory_space=pltpu.VMEM), pl.BlockSpec(memory_space=pltpu.HBM)
    block = 2 * tile * tile * HEAD_DIM * heads
    params = pltpu.CompilerParams(vmem_limit_bytes=VMEM_BYTES)
    by_row = (2, rows_dev, face, width)
    grad_query, own_grads, face_1_grads, face_2_grads, stats = pl.pallas_call(
        functools.partial(query_kernel, n_tm, n_height),
        out_shape=(
            jax.ShapeDtypeStruct((tile, width), bf16),
            jax.ShapeDtypeStruct((2, tile, width), f32),
            jax.ShapeDtypeStruct((2, face, width), bf16),
            jax.ShapeDtypeStruct((2, face, width), bf16),
            jax.ShapeDtypeStruct((1 + 2 * REACH, heads, tile), f32),
        ),
        in_specs=[vmem] * 2 + [hbm] * 6 + [pl.BlockSpec(memory_space=pltpu.SMEM)],
        out_specs=[vmem] * 5,
        scratch_shapes=[
            pltpu.VMEM((2, tile * (1 + n_picks) + 2 * face, 2 * HEAD_DIM), f32),
            pltpu.VMEM((2, tile * (1 + n_picks) + 2 * face, 2 * HEAD_DIM), bf16),
            *[pltpu.VMEM((2, face, width), bf16)] * 2,
            pltpu.VMEM((2 * REACH, 2, tile, width), bf16),
            stream_sems(heads, 2 + 2 * REACH),
        ],
        compiler_params=params,
        cost_estimate=pl.CostEstimate(flops=200 * block, bytes_accessed=4 << 20, transcendentals=0),
        name="query_side",
    )(query_grad, key_value, in_hbm(face_1.reshape(by_row)), in_hbm(face_2.reshape(by_row)),
      in_hbm(kv_part), in_hbm(kv_a), in_hbm(kv_b), in_hbm(kv_outer),
      far_picks.reshape(heads, n_picks))

    of_part, of_a = move(stats, partner), move(stats, route_a)
    of_b = move(jnp.stack([stats, of_part]), route_b)
    if not relayed:
        of_b = jnp.stack([of_b[0], move(stats, outer)])
    back_1 = lax.ppermute(face_1_grads, "height", pairs_1)
    back_2 = lax.ppermute(face_2_grads, "height", pairs_2)

    sums = pl.pallas_call(
        key_kernel,
        out_shape=jax.ShapeDtypeStruct((2, tile, width), f32),
        in_specs=[vmem] * 9,
        out_specs=vmem,
        scratch_shapes=[pltpu.VMEM((2, 3, tile, 2 * HEAD_DIM), f32)],
        compiler_params=params,
        cost_estimate=pl.CostEstimate(flops=80 * block, bytes_accessed=4 << 20, transcendentals=0),
        name="key_side",
    )(key_value, own_grads, back_1, back_2, qg_part, qg_b, qg_outer, of_part, of_b)
    grad_key, grad_value = pl.pallas_call(
        last_kernel,
        out_shape=(jax.ShapeDtypeStruct((tile, width), bf16),) * 2,
        in_specs=[vmem] * 4,
        out_specs=[vmem] * 2,
        scratch_shapes=[pltpu.VMEM((4, 1, tile, 2 * HEAD_DIM), f32)],
        compiler_params=params,
        cost_estimate=pl.CostEstimate(flops=30 * block, bytes_accessed=4 << 20, transcendentals=0),
        name="last_side",
    )(key_value, sums, qg_a, of_a)
    return tuple(x.reshape(query_tok.shape) for x in (grad_query, grad_key, grad_value))


def solution(mesh):
    spec = P("tm", "height", None, None)
    return jax.shard_map(
        per_device, mesh=mesh, in_specs=(spec,) * 5, out_specs=(spec,) * 3, check_vma=False
    )
```
